256 devices in a mesh: dp: 4 (over x), seq: 64 (over y, z, core).
Axes of the slice: x: 4, y: 4, z: 8, core: 2. Of those that a mesh axis runs over, the one named last changes fastest.
Arguments:
- activations: bfloat16 [4, 16384, 2048], P('dp', 'seq'), may hold values from -16 to 16
- w_query: bfloat16 [2048, 2048], replicated, may hold values from -0.125 to 0.125
- all_keys: bfloat16 [4, 16384, 2048], P('dp', 'seq'), may hold values from -6 to 6
- values: bfloat16 [4, 16384, 2048], P('dp', 'seq'), may hold values from -6 to 6
- grad_out: bfloat16 [4, 16384, 2048], P('dp', 'seq'), may hold values from -0.125 to 0.125
- cluster: int32 [4, 16384, 16], P('dp', 'seq'), may hold values from 0 to 255, as said below
Outputs:
- grad_query_weight: float32 [2048, 2048], P(('dp', 'seq'))
The draws below stay inside these ranges and needn't reach their ends.
Inputs may be any that keep to these rules, and one draw needn't show every extreme that they name: In every sequence and head, at most 2 of the 256 tokens of one device fall in one cluster, so a cluster holds at most 128 tokens. In every sequence there is a device index o along seq such that in every head each cluster whose number is o plus a multiple of the seq axis's device count holds exactly 2 tokens of every device.
All inputs are finite; a program needn't handle non-finite values.
Results may differ from the reference program's by a relative error of at most 0.0071.
Values may be sent and summed in bfloat16 or wider, within the bound.
No kernel may reach another device: no remote copies, remote signals or barrier semaphores. Data moves between devices by JAX's collectives and lax.ppermute only.
A program may use at most 128 MiB of HBM per device.

```python
import math
import jax
import jax.numpy as jnp
from jax import lax

D = 2048
H = 16
HS = 128
BLOCK = 128
TOK_DEV = 256
SEQS = 4
SEQ_LEN = 16384
HD = 2048
MEAN_BLK = 4
CLUSTERS = 256
PER_DEV = 2


def draw_cluster(key, part):
    key = jax.random.fold_in(key, 7)
    device_count = CLUSTERS // MEAN_BLK
    slot_count = PER_DEV * CLUSTERS
    key_busy, key_rest = jax.random.split(key)
    busy_owner = jax.random.randint(key_busy, (SEQS,), 0, device_count)
    slot_cluster = jnp.arange(slot_count) // PER_DEV
    key_table = jax.random.split(key_rest, SEQS * H * device_count)

    def draw_rows(key_row, owner_now):
        key_pick, key_order = jax.random.split(key_row)
        scores = jax.random.permutation(key_pick, slot_count)
        forced = slot_cluster % device_count == owner_now
        scores = jnp.where(forced, scores - slot_count, scores)
        chosen = jnp.argsort(scores, stable=True)[:TOK_DEV]
        picked = slot_cluster[chosen]
        order = jax.random.permutation(key_order, TOK_DEV)
        return picked[order]
    owner_rep = jnp.repeat(busy_owner, H * device_count)
    drawn = jax.vmap(draw_rows)(key_table, owner_rep).reshape(SEQS, H, device_count, TOK_DEV)
    return drawn.transpose(0, 2, 3, 1).reshape(SEQS, SEQ_LEN, H).astype(jnp.int32)


def with_spikes(array, rng, source, target, shards_of, factor):
    owner, partner = [(jnp.arange(array.shape[dim]) // (array.shape[dim] // shards_of)).reshape([-1 if axis == dim else 1 for axis in range(array.ndim)]) for dim in (source, target)]
    chosen = jax.random.permutation(rng, shards_of)[partner]
    strong = (owner == chosen) | (owner == (partner + shards_of // 2) % shards_of)
    return jnp.where(strong, factor * array, array)


def level_of(stream_key, shape, pieces, low, top_value):
    loudness, own = 1.0, jax.random.fold_in(stream_key, 6)
    for dim, shards_of in pieces:
        steps = jnp.exp(jax.random.uniform(jax.random.fold_in(own, dim), (shards_of,), jnp.float32, low / len(pieces), top_value / len(pieces)))
        loudness = loudness * jnp.repeat(steps, shape[dim] // shards_of).reshape([-1 if axis == dim else 1 for axis in range(len(shape))])
    return loudness


def gaussian(rng, dims, width, bound, cuts=(), kind=jnp.bfloat16):
    result = width * jax.random.normal(rng, dims, jnp.float32)
    if cuts:
        result = result * level_of(rng, dims, cuts, -0.22, 0.18)
    return jnp.clip(result, -bound, bound).astype(kind)


def bell_draw_with(rng, dims, width, bound, cuts, heavy, kind=jnp.bfloat16):
    array = width * jax.random.normal(rng, dims, jnp.float32)
    if cuts:
        array = array * level_of(rng, dims, cuts, -0.22, 0.18)
    return jnp.clip(with_spikes(array, jax.random.fold_in(rng, 3), *heavy), -bound, bound).astype(kind)


def setup_inputs(seed: int = 0) -> dict:
    key_of = jax.random.split(jax.random.key(seed), 7)
    activations = bell_draw_with(key_of[0], (SEQS, SEQ_LEN, D), 1.0, 16.0, ((0, 4), (1, 64)), (1, 2, 64, 4.0))
    w_query = gaussian(key_of[1], (D, HD), D ** -0.5, 0.125)
    all_keys = gaussian(key_of[2], (SEQS, SEQ_LEN, HD), 1.0, 6.0, ((0, 4), (1, 64)))
    values = gaussian(key_of[3], (SEQS, SEQ_LEN, HD), 1.0, 6.0, ((0, 4), (1, 64)))
    grad_out = gaussian(key_of[4], (SEQS, SEQ_LEN, HD), 0.02, 0.125, ((0, 4), (1, 64)))
    cluster = draw_cluster(jax.random.fold_in(key_of[6], 71), 0)
    return dict(activations=activations, w_query=w_query, all_keys=all_keys, values=values, grad_out=grad_out, cluster=cluster)


def block_grads(query_rows, key_rows, value_rows, grad_rows, assign):
    onehot = (assign[:, None] == jnp.arange(CLUSTERS)[None, :]).astype(jnp.int32)
    ranked = lax.optimization_barrier(jnp.sum((jnp.cumsum(onehot, axis=0) - onehot) * onehot, axis=1)).astype(jnp.int32)

    def place(data):
        return jnp.zeros((CLUSTERS, BLOCK, data.shape[-1]), data.dtype).at[assign, ranked].set(data)
    query_blk = place(query_rows).astype(jnp.float32)
    key_blk = place(key_rows).astype(jnp.float32)
    value_blk = place(value_rows).astype(jnp.float32)
    grad_blk = place(grad_rows).astype(jnp.float32)
    scale = 1.0 / math.sqrt(HS)
    position = jnp.arange(BLOCK)
    causal = position[:, None] >= position[None, :]
    scores = jnp.einsum('nqd,nkd->nqk', query_blk, key_blk) * scale
    raised = jnp.where(causal, jnp.exp(scores), 0.0)
    weights = raised / lax.optimization_barrier(jnp.sum(raised, axis=-1, keepdims=True))
    weights_low = lax.optimization_barrier(weights.astype(jnp.bfloat16)).astype(jnp.float32)
    attended = jnp.einsum('nqk,nkd->nqd', weights_low, value_blk)
    dweights = jnp.einsum('nqd,nkd->nqk', grad_blk, value_blk)
    delta = lax.optimization_barrier(jnp.sum(grad_blk * attended, axis=-1, keepdims=True))
    dscores = lax.optimization_barrier((weights * (dweights - delta)).astype(jnp.bfloat16)).astype(jnp.float32)
    dquery = (jnp.einsum('nqk,nkd->nqd', dscores, key_blk) * scale).astype(jnp.bfloat16)
    return dquery[assign, ranked]

def heads_major(data):
    return data.reshape(SEQS, SEQ_LEN, H, HS).transpose(0, 2, 1, 3).reshape(SEQS * H, SEQ_LEN, HS)

def one_head(bundle):
    return block_grads(bundle[0], bundle[1], bundle[2], bundle[3], bundle[4])

def reference(activations, w_query, all_keys, values, grad_out, cluster):
    queries = jnp.dot(activations, w_query, preferred_element_type=jnp.float32).astype(jnp.bfloat16)
    assign = cluster.transpose(0, 2, 1).reshape(SEQS * H, SEQ_LEN)
    dquery = lax.map(one_head, (heads_major(queries), heads_major(all_keys), heads_major(values), heads_major(grad_out), assign))
    dquery = dquery.reshape(SEQS, H, SEQ_LEN, HS).transpose(0, 2, 1, 3).reshape(SEQS, SEQ_LEN, H * HS)
    total = jnp.zeros((D, H * HS), jnp.float32)
    for seq_index in range(SEQS):
        total = total + jnp.dot(activations[seq_index].T, dquery[seq_index], preferred_element_type=jnp.float32)
    return total
```

```python
import functools
import math

import jax
import jax.numpy as jnp
from jax import lax
from jax.experimental import pallas as pl
from jax.experimental.pallas import tpu as pltpu
from jax.sharding import PartitionSpec as P

HEAD = 128
TOK = 256
OWNERS = 64
CELL = 8
SLOTS = OWNERS * CELL
HEADS = 16
CHUNKS = 2
HPC = HEADS // CHUNKS
EMPTY = 128.0
VMEM = 48 * 1024 * 1024
BF = jnp.bfloat16
F32 = jnp.float32


def dot(a, b, dims):
    return lax.dot_general(a, b, (dims, ((), ())), preferred_element_type=F32)


NN = ((1,), (0,))
NT = ((1,), (1,))


def params(*semantics):
    return pltpu.CompilerParams(vmem_limit_bytes=VMEM, dimension_semantics=semantics or None)


def slot_kernel(col_ref, row_ref, out_ref):
    earlier = lax.broadcasted_iota(jnp.int32, (TOK, TOK), 0) < lax.broadcasted_iota(
        jnp.int32, (TOK, TOK), 1
    )
    for h in range(HEADS):
        row = row_ref[h : h + 1, :]
        same = (col_ref[:, h : h + 1] == row) & earlier
        rank = jnp.sum(jnp.where(same, 1, 0), axis=0, keepdims=True)
        out_ref[h : h + 1, :] = (row % OWNERS) * CELL + (row // OWNERS) * 2 + rank


def slots_of(assign):
    return pl.pallas_call(
        slot_kernel,
        out_shape=jax.ShapeDtypeStruct((HEADS, TOK), jnp.int32),
        compiler_params=params(),
        name="slots",
    )(assign, assign.T)


def pack_kernel(mark, slot_ref, *refs):
    sources, out_ref = refs[:-1], refs[-1]
    place = lax.broadcasted_iota(jnp.int32, (SLOTS, TOK), 0)
    for n, source in enumerate(sources):
        parts = []
        for e in range(2):
            hot = jnp.where(place == slot_ref[0, e : e + 1, :], 1.0, 0.0)
            hot_low = hot.astype(BF)
            rows = dot(hot_low, source[:, e * HEAD : (e + 1) * HEAD], NN)
            if mark and n == 0:
                filled = dot(hot_low, jnp.ones((TOK, HEAD), BF), NN)
                rows = jnp.where(filled > 0.5, rows, EMPTY)
            parts.append(rows.reshape(OWNERS, CELL, HEAD))
        out_ref[:, :, n * HEAD : (n + 1) * HEAD] = jnp.concatenate(parts, axis=1).astype(BF)


def pack(slots, chunk, mark, *sources):
    pairs = HPC // 2
    width = HEAD * len(sources)
    return pl.pallas_call(
        functools.partial(pack_kernel, mark),
        grid=(pairs,),
        in_specs=[pl.BlockSpec((1, 2, TOK), lambda p: (chunk * pairs + p, 0, 0))]
        + [pl.BlockSpec((TOK, 2 * HEAD), lambda p: (0, chunk * pairs + p)) for _ in sources],
        out_specs=pl.BlockSpec((OWNERS, 2 * CELL, width), lambda p: (0, p, 0)),
        out_shape=jax.ShapeDtypeStruct((OWNERS, HPC * CELL, width), BF),
        compiler_params=params("arbitrary"),
        cost_estimate=pl.CostEstimate(
            flops=2 * HPC * SLOTS * TOK * width * 4, bytes_accessed=6 * 2**20, transcendentals=0
        ),
        name="pack",
    )(slots.reshape(HEADS // 2, 2, TOK), *sources)


def attention_kernel(kvg_ref, q_ref, out_ref, bias_ref):
    scale = 1.0 / math.sqrt(HEAD)
    to_exp2 = scale * math.log2(math.e)

    @pl.when(pl.program_id(0) == 0)
    def _():
        row = lax.broadcasted_iota(jnp.int32, (SLOTS, SLOTS), 0)
        col = lax.broadcasted_iota(jnp.int32, (SLOTS, SLOTS), 1)
        keep = (col <= row) & ((row % CELL) // 2 == (col % CELL) // 2)
        bias_ref[...] = jnp.where(keep, 0.0, -1e30)

    first = jnp.where(lax.broadcasted_iota(jnp.int32, (8, HEAD), 1) == 0, 1.0, 0.0).astype(BF)
    kvg_pair = kvg_ref[...].astype(F32)
    q_pair = q_ref[...].astype(F32)
    step = 128
    for e in range(2):
        kvg = kvg_pair[:, e * CELL : (e + 1) * CELL, :].reshape(SLOTS, 3 * HEAD).astype(BF)
        q = q_pair[:, e * CELL : (e + 1) * CELL, :].reshape(SLOTS, HEAD).astype(BF)
        k, v, g = (kvg[:, n * HEAD : (n + 1) * HEAD] for n in range(3))
        key_bias = jnp.where(dot(first, k, NT)[0:1, :] > 0.5 * EMPTY, -1e30, 0.0)
        for i in range(SLOTS // step):
            here = slice(i * step, (i + 1) * step)
            n = (i + 1) * step
            score = dot(q[here], k[:n], NT) * to_exp2 + bias_ref[here, :n] + key_bias[:, :n]
            raised = jnp.exp2(score)
            total = jnp.sum(raised, axis=1, keepdims=True)
            weights = raised * (1.0 / jnp.where(total == 0.0, 1.0, total))
            attended = dot(weights.astype(BF), v[:n], NN)
            dweights = dot(g[here], v[:n], NT)
            delta = jnp.sum(g[here].astype(F32) * attended, axis=1, keepdims=True)
            dscores = (weights * (dweights - delta)).astype(BF)
            dquery = (dot(dscores, k[:n], NN) * scale).astype(BF)
            tiles = step // (2 * CELL)
            out_ref[0, i * tiles : (i + 1) * tiles, e] = dquery.reshape(tiles, 2 * CELL, HEAD)


def attention(kvg, q):
    return pl.pallas_call(
        attention_kernel,
        grid=(HPC // 2,),
        in_specs=[
            pl.BlockSpec((OWNERS, 2 * CELL, 3 * HEAD), lambda p: (0, p, 0)),
            pl.BlockSpec((OWNERS, 2 * CELL, HEAD), lambda p: (0, p, 0)),
        ],
        out_specs=pl.BlockSpec((1, OWNERS // 2, 2, 2 * CELL, HEAD), lambda p: (p, 0, 0, 0, 0)),
        out_shape=jax.ShapeDtypeStruct((HPC // 2, OWNERS // 2, 2, 2 * CELL, HEAD), BF),
        scratch_shapes=[pltpu.VMEM((SLOTS, SLOTS), F32)],
        compiler_params=params("arbitrary"),
        cost_estimate=pl.CostEstimate(
            flops=HPC * 8 * SLOTS * SLOTS * HEAD,
            bytes_accessed=5 * 2**20,
            transcendentals=HPC * SLOTS * SLOTS,
        ),
        name="attention",
    )(kvg, q)


def grad_kernel(where_ref, rows_ref, slot_a, slot_b, act_a, act_b, out_ref, acc_ref):
    b = pl.program_id(0)
    head, core = where_ref[0], where_ref[1]
    rows = rows_ref[...].reshape(OWNERS * 2 * CELL, HEAD)
    lane = lax.broadcasted_iota(jnp.int32, (TOK, HEADS), 1)
    place = lax.broadcasted_iota(jnp.int32, (TOK, OWNERS * 2 * CELL), 1)
    total = None
    for slot_ref, act_ref, side in ((slot_a, act_a, core), (slot_b, act_b, 1 - core)):
        slot = jnp.sum(jnp.where(lane == head, slot_ref[0], 0), axis=1, keepdims=True)
        index = (slot // CELL) * (2 * CELL) + side * CELL + slot % CELL
        hot = jnp.where(place == index, 1.0, 0.0).astype(BF)
        dquery = dot(hot, rows, NN).astype(BF)
        term = dot(act_ref[0], dquery, NN)
        total = term if total is None else total + term

    @pl.when(b == 0)
    def _():
        acc_ref[...] = total

    @pl.when(b > 0)
    def _():
        acc_ref[...] += total

    @pl.when(b == pl.num_programs(0) - 1)
    def _():
        out_ref[...] = acc_ref[...].astype(BF)


def weight_grad(where, rows, slots, acts, features, seqs):
    def slot_spec():
        return pl.BlockSpec((1, TOK, HEADS), lambda b, w: (b, 0, 0))

    def act_spec():
        return pl.BlockSpec((1, features, TOK), lambda b, w: (b, 0, 0))

    return pl.pallas_call(
        grad_kernel,
        grid_spec=pltpu.PrefetchScalarGridSpec(
            num_scalar_prefetch=1,
            grid=(seqs,),
            in_specs=[
                pl.BlockSpec((OWNERS, 2 * CELL, HEAD), lambda b, w: (b, 0, 0)),
                slot_spec(),
                slot_spec(),
                act_spec(),
                act_spec(),
            ],
            out_specs=pl.BlockSpec((features, HEAD), lambda b, w: (0, 0)),
            scratch_shapes=[pltpu.VMEM((features, HEAD), F32)],
        ),
        out_shape=jax.ShapeDtypeStruct((features, HEAD), BF),
        compiler_params=params("arbitrary"),
        cost_estimate=pl.CostEstimate(
            flops=4 * seqs * TOK * features * HEAD * 2,
            bytes_accessed=12 * 2**20,
            transcendentals=0,
        ),
        name="weight_grad",
    )(where, rows, *slots, *acts)


def on_device(activations, w_query, all_keys, values, grad_out, cluster):
    tokens_here = activations[0]
    features = tokens_here.shape[1]
    seqs = lax.axis_size("dp")
    devices = seqs * OWNERS
    slots = slots_of(cluster[0])
    seq_send = functools.partial(
        lax.all_to_all, axis_name="seq", split_axis=0, concat_axis=0, tiled=True
    )
    all_send = functools.partial(
        lax.all_to_all, axis_name=("dp", "seq"), split_axis=0, concat_axis=0, tiled=True
    )
    kvg = [pack(slots, c, True, all_keys[0], values[0], grad_out[0]) for c in range(CHUNKS)]
    queries = jnp.dot(tokens_here, w_query, preferred_element_type=F32).astype(BF)
    q = [pack(slots, c, False, queries) for c in range(CHUNKS)]

    swap = [(i, i ^ 1) for i in range(OWNERS)]
    acts_mine = lax.all_gather(tokens_here.T, "dp")
    slots_mine = lax.all_gather(slots.T, "dp")
    acts = (acts_mine, lax.ppermute(acts_mine, "seq", swap))
    slot_cols = (slots_mine, lax.ppermute(slots_mine, "seq", swap))
    core = lax.axis_index("seq") % 2
    group = lax.axis_index("dp") * 2 + core

    sums = []
    for c in range(CHUNKS):
        got_kvg, got_q = seq_send(kvg[c]), seq_send(q[c])
        rows = attention(got_kvg, got_q)
        rows = rows.reshape(HPC // 2, OWNERS // 2, 2, 2 * CELL, HEAD)
        back = all_send(rows.reshape(devices, 2 * CELL, HEAD))
        where = jnp.stack([c * HPC + group, core]).astype(jnp.int32)
        part = weight_grad(where, back, slot_cols, acts, features, seqs)
        got = all_send(part.reshape(devices, features // devices, HEAD))
        got = got.reshape(seqs, OWNERS // 2, 2, features // devices, HEAD)
        total = jnp.sum(got.astype(F32), axis=1)
        sums.append(total.reshape(HPC, features // devices, HEAD))
    out = jnp.concatenate(sums, axis=0)
    return out.transpose(1, 0, 2).reshape(features // devices, HEADS * HEAD)


def solution(mesh):
    placed = (
        P("dp", "seq", None),
        P(),
        P("dp", "seq", None),
        P("dp", "seq", None),
        P("dp", "seq", None),
        P("dp", "seq", None),
    )
    return jax.shard_map(
        on_device, mesh=mesh, in_specs=placed, out_specs=P(("dp", "seq"), None), check_vma=False
    )
```

```python
import functools
import math

import jax
import jax.numpy as jnp
from jax import lax
from jax.experimental import pallas as pl
from jax.experimental.pallas import tpu as pltpu
from jax.sharding import PartitionSpec as P

HEAD = 128
TOK = 256
OWNERS = 64
CELL = 8
SLOTS = OWNERS * CELL
HEADS = 16
CHUNKS = 2
HPC = HEADS // CHUNKS
EMPTY = 128.0
VMEM = 48 * 1024 * 1024
BF = jnp.bfloat16
F32 = jnp.float32


def dot(a, b, dims):
    return lax.dot_general(a, b, (dims, ((), ())), preferred_element_type=F32)


NN = ((1,), (0,))
NT = ((1,), (1,))


def params(*semantics):
    return pltpu.CompilerParams(vmem_limit_bytes=VMEM, dimension_semantics=semantics or None)


def slot_kernel(col_ref, row_ref, out_ref):
    earlier = lax.broadcasted_iota(jnp.int32, (TOK, TOK), 0) < lax.broadcasted_iota(
        jnp.int32, (TOK, TOK), 1
    )
    for h in range(HEADS):
        row = row_ref[h : h + 1, :]
        same = (col_ref[:, h : h + 1] == row) & earlier
        rank = jnp.sum(jnp.where(same, 1, 0), axis=0, keepdims=True)
        out_ref[h : h + 1, :] = (row % OWNERS) * CELL + (row // OWNERS) * 2 + rank


def slots_of(assign):
    return pl.pallas_call(
        slot_kernel,
        out_shape=jax.ShapeDtypeStruct((HEADS, TOK), jnp.int32),
        compiler_params=params(),
        name="slots",
    )(assign, assign.T)


def pack_kernel(mark, slot_ref, *refs):
    sources, out_ref = refs[:-1], refs[-1]
    place = lax.broadcasted_iota(jnp.int32, (SLOTS, TOK), 0)
    for n, source in enumerate(sources):
        parts = []
        for e in range(2):
            hot = jnp.where(place == slot_ref[0, e : e + 1, :], 1.0, 0.0)
            hot_low = hot.astype(BF)
            rows = dot(hot_low, source[:, e * HEAD : (e + 1) * HEAD], NN)
            if mark and n == 0:
                filled = dot(hot_low, jnp.ones((TOK, HEAD), BF), NN)
                rows = jnp.where(filled > 0.5, rows, EMPTY)
            parts.append(rows.reshape(OWNERS, CELL, HEAD))
        out_ref[:, :, n * HEAD : (n + 1) * HEAD] = jnp.concatenate(parts, axis=1).astype(BF)


def pack(slots, chunk, mark, *sources):
    pairs = HPC // 2
    width = HEAD * len(sources)
    return pl.pallas_call(
        functools.partial(pack_kernel, mark),
        grid=(pairs,),
        in_specs=[pl.BlockSpec((1, 2, TOK), lambda p: (chunk * pairs + p, 0, 0))]
        + [pl.BlockSpec((TOK, 2 * HEAD), lambda p: (0, chunk * pairs + p)) for _ in sources],
        out_specs=pl.BlockSpec((OWNERS, 2 * CELL, width), lambda p: (0, p, 0)),
        out_shape=jax.ShapeDtypeStruct((OWNERS, HPC * CELL, width), BF),
        compiler_params=params("arbitrary"),
        cost_estimate=pl.CostEstimate(
            flops=2 * HPC * SLOTS * TOK * width * 4, bytes_accessed=6 * 2**20, transcendentals=0
        ),
        name="pack",
    )(slots.reshape(HEADS // 2, 2, TOK), *sources)


def attention_kernel(in_ref, out_ref, bias_ref):
    scale = 1.0 / math.sqrt(HEAD)
    to_exp2 = scale * math.log2(math.e)

    @pl.when(pl.program_id(0) == 0)
    def _():
        row = lax.broadcasted_iota(jnp.int32, (SLOTS, SLOTS), 0)
        col = lax.broadcasted_iota(jnp.int32, (SLOTS, SLOTS), 1)
        keep = (col <= row) & ((row % CELL) // 2 == (col % CELL) // 2)
        bias_ref[...] = jnp.where(keep, 0.0, -1e30)

    first = jnp.where(lax.broadcasted_iota(jnp.int32, (8, HEAD), 1) == 0, 1.0, 0.0).astype(BF)
    pair = in_ref[...].astype(F32)
    step = 256
    for e in range(2):
        rows = pair[:, e * CELL : (e + 1) * CELL, :].reshape(SLOTS, 4 * HEAD).astype(BF)
        k, v, g, q = (rows[:, n * HEAD : (n + 1) * HEAD] for n in range(4))
        key_bias = jnp.where(dot(first, k, NT)[0:1, :] > 0.5 * EMPTY, -1e30, 0.0)
        for i in range(SLOTS // step):
            here = slice(i * step, (i + 1) * step)
            n = (i + 1) * step
            score = dot(q[here], k[:n], NT) * to_exp2 + bias_ref[here, :n] + key_bias[:, :n]
            raised = jnp.exp2(score)
            total = jnp.sum(raised, axis=1, keepdims=True)
            weights = raised * (1.0 / jnp.where(total == 0.0, 1.0, total))
            attended = dot(weights.astype(BF), v[:n], NN)
            dweights = dot(g[here], v[:n], NT)
            delta = jnp.sum(g[here].astype(F32) * attended, axis=1, keepdims=True)
            dscores = (weights * (dweights - delta)).astype(BF)
            dquery = (dot(dscores, k[:n], NN) * scale).astype(BF)
            tiles = step // (2 * CELL)
            out_ref[0, i * tiles : (i + 1) * tiles, e] = dquery.reshape(tiles, 2 * CELL, HEAD)


def attention(got):
    return pl.pallas_call(
        attention_kernel,
        grid=(HPC // 2,),
        in_specs=[pl.BlockSpec((OWNERS, 2 * CELL, 4 * HEAD), lambda p: (0, p, 0))],
        out_specs=pl.BlockSpec((1, OWNERS // 2, 2, 2 * CELL, HEAD), lambda p: (p, 0, 0, 0, 0)),
        out_shape=jax.ShapeDtypeStruct((HPC // 2, OWNERS // 2, 2, 2 * CELL, HEAD), BF),
        scratch_shapes=[pltpu.VMEM((SLOTS, SLOTS), F32)],
        compiler_params=params("arbitrary"),
        cost_estimate=pl.CostEstimate(
            flops=HPC * 8 * SLOTS * SLOTS * HEAD,
            bytes_accessed=5 * 2**20,
            transcendentals=HPC * SLOTS * SLOTS,
        ),
        name="attention",
    )(got)


def grad_kernel(where_ref, rows_ref, act_a, act_b, *refs):
    earlier_ref, out_ref, acc_ref = refs if len(refs) == 3 else (None, *refs)
    b = pl.program_id(0)
    head, core = where_ref[0], where_ref[1]
    features = acc_ref.shape[0]
    rows = rows_ref[...].reshape(OWNERS * 2 * CELL, HEAD)
    line = lax.broadcasted_iota(jnp.int32, (2 * HEADS, TOK), 0)
    place = lax.broadcasted_iota(jnp.int32, (OWNERS * 2 * CELL, TOK), 0)
    total = None
    for act_ref, side in ((act_a, core), (act_b, 1 - core)):
        slot = act_ref[0, features:, :].astype(F32)
        weight = jnp.where(line == head, 2.0 * CELL, jnp.where(line == HEADS + head, 1.0, 0.0))
        index = jnp.sum(slot * weight, axis=0, keepdims=True).astype(jnp.int32) + side * CELL
        hot = jnp.where(place == index, 1.0, 0.0).astype(BF)
        dquery = dot(rows, hot, ((0,), (0,))).astype(BF)
        term = dot(act_ref[0, :features, :], dquery, NT)
        total = term if total is None else total + term

    @pl.when(b == 0)
    def _():
        acc_ref[...] = total

    @pl.when(b > 0)
    def _():
        acc_ref[...] += total

    @pl.when(b == pl.num_programs(0) - 1)
    def _():
        if earlier_ref is None:
            out_ref[...] = acc_ref[...]
        else:
            both = [ref[...].reshape(-1, CELL, HEAD) for ref in (earlier_ref, acc_ref)]
            out_ref[...] = jnp.concatenate(both, axis=1).astype(BF)


def weight_grad(where, rows, acts, features, seqs, earlier):
    def act_spec():
        return pl.BlockSpec((1, features + 2 * HEADS, TOK), lambda b, w: (b, 0, 0))

    in_specs = [
        pl.BlockSpec((OWNERS, 2 * CELL, HEAD), lambda b, w: (b, 0, 0)),
        act_spec(),
        act_spec(),
    ]
    if earlier is None:
        out = jax.ShapeDtypeStruct((features, HEAD), F32)
        out_spec = pl.BlockSpec((features, HEAD), lambda b, w: (0, 0))
        more = ()
    else:
        out = jax.ShapeDtypeStruct((features // CELL, 2 * CELL, HEAD), BF)
        out_spec = pl.BlockSpec((features // CELL, 2 * CELL, HEAD), lambda b, w: (0, 0, 0))
        in_specs.append(pl.BlockSpec((features, HEAD), lambda b, w: (0, 0)))
        more = (earlier,)
    return pl.pallas_call(
        grad_kernel,
        grid_spec=pltpu.PrefetchScalarGridSpec(
            num_scalar_prefetch=1,
            grid=(seqs,),
            in_specs=in_specs,
            out_specs=out_spec,
            scratch_shapes=[pltpu.VMEM((features, HEAD), F32)],
        ),
        out_shape=out,
        compiler_params=params("arbitrary"),
        cost_estimate=pl.CostEstimate(
            flops=4 * seqs * TOK * features * HEAD * 2,
            bytes_accessed=12 * 2**20,
            transcendentals=0,
        ),
        name="weight_grad",
    )(where, rows, *acts, *more)


def on_device(activations, w_query, all_keys, values, grad_out, cluster):
    tokens_here = activations[0]
    features = tokens_here.shape[1]
    seqs = lax.axis_size("dp")
    devices = seqs * OWNERS
    slots = slots_of(cluster[0])
    seq_send = functools.partial(
        lax.all_to_all, axis_name="seq", split_axis=0, concat_axis=0, tiled=True
    )
    all_send = functools.partial(
        lax.all_to_all, axis_name=("dp", "seq"), split_axis=0, concat_axis=0, tiled=True
    )
    queries = jnp.dot(tokens_here, w_query, preferred_element_type=F32).astype(BF)
    sent = [
        pack(slots, c, True, all_keys[0], values[0], grad_out[0], queries) for c in range(CHUNKS)
    ]

    swap = [(i, i ^ 1) for i in range(OWNERS)]
    carried = jnp.concatenate(
        [tokens_here.T, (slots // CELL).astype(BF), (slots % CELL).astype(BF)], axis=0
    )
    acts_mine = lax.all_gather(carried, "dp")
    acts = (acts_mine, lax.ppermute(acts_mine, "seq", swap))
    core = lax.axis_index("seq") % 2
    group = lax.axis_index("dp") * 2 + core

    got, last = [], None
    for c in range(CHUNKS):
        block = sent[c]
        if last is not None:
            block, got[-1] = lax.optimization_barrier((block, last))
        last = seq_send(block)
        got.append(last)
    part = None
    for c in range(CHUNKS):
        rows = attention(got[c])
        back = all_send(rows.reshape(devices, 2 * CELL, HEAD))
        where = jnp.stack([c * HPC + group, core]).astype(jnp.int32)
        part = weight_grad(where, back, acts, features, seqs, part)
    terms = all_send(part)
    terms = terms.reshape(seqs, OWNERS // 2, 2, CHUNKS, features // devices, HEAD)
    out = jnp.sum(terms.astype(F32), axis=1)
    out = out.transpose(3, 2, 0, 1, 4)
    return out.reshape(features // devices, HEADS * HEAD)


def solution(mesh):
    placed = (
        P("dp", "seq", None),
        P(),
        P("dp", "seq", None),
        P("dp", "seq", None),
        P("dp", "seq", None),
        P("dp", "seq", None),
    )
    return jax.shard_map(
        on_device, mesh=mesh, in_specs=placed, out_specs=P(("dp", "seq"), None), check_vma=False
    )
```

```python
import functools
import math

import jax
import jax.numpy as jnp
from jax import lax
from jax.experimental import pallas as pl
from jax.experimental.pallas import tpu as pltpu
from jax.sharding import PartitionSpec as P

HEAD = 128
TOK = 256
OWNERS = 64
CELL = 8
SLOTS = OWNERS * CELL
HEADS = 16
CARRIED = 2 * HEADS
CHUNKS = 2
HPC = HEADS // CHUNKS
COMPACT = 96
GROUP = 16
FILLS = 4
EMPTY = 128.0
VMEM = 48 * 1024 * 1024
BF = jnp.bfloat16
F32 = jnp.float32


def dot(a, b, dims):
    return lax.dot_general(a, b, (dims, ((), ())), preferred_element_type=F32)


NN = ((1,), (0,))
NT = ((1,), (1,))


def params(*semantics, vmem=VMEM):
    return pltpu.CompilerParams(vmem_limit_bytes=vmem, dimension_semantics=semantics or None)


def slot_kernel(col_ref, row_ref, out_ref, held_ref, row_of_ref, over_ref):
    earlier = lax.broadcasted_iota(jnp.int32, (TOK, TOK), 0) < lax.broadcasted_iota(
        jnp.int32, (TOK, TOK), 1
    )
    owners = lax.broadcasted_iota(jnp.int32, (OWNERS, TOK), 0)
    lanes = lax.broadcasted_iota(jnp.int32, (HEADS * CELL, TOK), 0)
    held = None
    for h in range(HEADS):
        row = row_ref[h : h + 1, :]
        same = (col_ref[:, h : h + 1] == row) & earlier
        rank = jnp.sum(jnp.where(same, 1, 0), axis=0, keepdims=True)
        owner = (row + 4 * h + row // OWNERS) % OWNERS
        cell = (row // OWNERS) * 2 + rank
        out_ref[h : h + 1, :] = owner * CELL + cell
        to_owner = jnp.where(owners == owner, 1.0, 0.0).astype(BF)
        to_lane = jnp.where(lanes == h * CELL + cell, 1.0, 0.0).astype(BF)
        term = dot(to_owner, to_lane, NT)
        held = term if held is None else held + term
    held_ref[...] = held
    before = lax.broadcasted_iota(jnp.int32, (HEADS * CELL, HEADS * CELL), 0) < (
        lax.broadcasted_iota(jnp.int32, (HEADS * CELL, HEADS * CELL), 1)
    )
    rank = dot(held.astype(BF), jnp.where(before, 1.0, 0.0).astype(BF), NN)
    row_of = jnp.where(held > 0.5, rank + 1.0, -1.0)
    row_of_ref[...] = row_of
    most = jnp.max(jnp.max(row_of, axis=0, keepdims=True), axis=1, keepdims=True)
    over_ref[...] = jnp.broadcast_to(jnp.where(most >= COMPACT, 1.0, 0.0), over_ref.shape)


def slots_of(assign):
    per_owner = jax.ShapeDtypeStruct((OWNERS, HEADS * CELL), F32)
    return pl.pallas_call(
        slot_kernel,
        out_shape=(
            jax.ShapeDtypeStruct((HEADS, TOK), jnp.int32),
            per_owner,
            per_owner,
            jax.ShapeDtypeStruct((8, HEAD), F32),
        ),
        compiler_params=params(),
        name="slots",
    )(assign, assign.T)


def compact_kernel(slot_ref, row_of_ref, held_ref, flag_ref, one_ref, two_ref, out_ref, buf_ref):
    p = pl.program_id(0)

    @pl.when(p < FILLS)
    def _():
        place = lax.broadcasted_iota(jnp.int32, (SLOTS, TOK), 0)
        for e in range(0, HEADS // FILLS, 2):
            parts = []
            for h in (e, e + 1):
                hot = jnp.where(place == slot_ref[0, h : h + 1, :], 1.0, 0.0).astype(BF)
                here = slice(h * HEAD, (h + 1) * HEAD)
                both = jnp.concatenate([one_ref[:, here], two_ref[:, here]], axis=1)
                parts.append(dot(hot, both, NN).reshape(OWNERS, CELL, 2 * HEAD))
            first = p * (HEADS // FILLS) * CELL + e * CELL
            at = pl.ds(pl.multiple_of(first, 2 * CELL), 2 * CELL)
            buf_ref[:, at, :] = jnp.concatenate(parts, axis=1).astype(BF)

    @pl.when(p >= FILLS)
    def _():
        first = pl.multiple_of((p - FILLS) * GROUP, GROUP)
        row_of = row_of_ref[pl.ds(first, GROUP), :]
        row_of = jnp.where(row_of < COMPACT, row_of, -2.0 * COMPACT).astype(jnp.int32)
        held = held_ref[pl.ds(first, GROUP), :]
        notes = jnp.concatenate([held, jnp.broadcast_to(flag_ref[0:1, :], held.shape)], axis=1)
        place = lax.broadcasted_iota(jnp.int32, (2 * COMPACT, 2 * HEAD), 0)
        line = lax.broadcasted_iota(jnp.int32, (2 * CELL, 2 * HEAD), 0)
        for d in range(0, GROUP, 2):
            target = jnp.concatenate([row_of[d : d + 1], row_of[d + 1 : d + 2] + COMPACT], axis=1)
            hot = jnp.where(place == target, 1.0, 0.0).astype(BF)
            rows = buf_ref[pl.ds(first + d, 2)].reshape(2 * HEADS * CELL, 2 * HEAD)
            block = dot(hot, rows, NN)
            for e in range(2):
                mine = block[e * COMPACT : (e + 1) * COMPACT]
                top = jnp.where(line == 0, notes[d + e : d + e + 1], mine[: 2 * CELL])
                out_ref[d + e] = jnp.concatenate([top, mine[2 * CELL :]], axis=0).astype(BF)


def compact(slots, row_of, held, flag, one, two):
    groups = OWNERS // GROUP
    share = HEADS // FILLS
    whole = pl.BlockSpec((OWNERS, HEADS * CELL), lambda p: (0, 0))
    source = pl.BlockSpec((TOK, share * HEAD), lambda p: (0, jnp.minimum(p, FILLS - 1)))
    return pl.pallas_call(
        compact_kernel,
        grid=(FILLS + groups,),
        in_specs=[
            pl.BlockSpec((1, share, TOK), lambda p: (jnp.minimum(p, FILLS - 1), 0, 0)),
            whole,
            whole,
            pl.BlockSpec((8, HEAD), lambda p: (0, 0)),
            source,
            source,
        ],
        out_specs=pl.BlockSpec(
            (GROUP, COMPACT, 2 * HEAD), lambda p: (jnp.maximum(p - FILLS, 0), 0, 0)
        ),
        out_shape=jax.ShapeDtypeStruct((OWNERS, COMPACT, 2 * HEAD), BF),
        scratch_shapes=[pltpu.VMEM((OWNERS, HEADS * CELL, 2 * HEAD), BF)],
        compiler_params=params("arbitrary", vmem=60 * 1024 * 1024),
        cost_estimate=pl.CostEstimate(
            flops=4 * 2**30, bytes_accessed=8 * 2**20, transcendentals=0
        ),
        name="compact",
    )(slots.reshape(FILLS, share, TOK), row_of, held, flag, one, two)


def spread_kernel(mark, got_ref, note_ref, out_ref):
    slots = HEADS * CELL
    row = lax.broadcasted_iota(jnp.int32, (slots, slots), 0)
    col = lax.broadcasted_iota(jnp.int32, (slots, slots), 1)
    held = note_ref[...].astype(F32)[:, 0, :HEAD].astype(BF)
    rank = dot(jnp.where(col < row, 1.0, 0.0).astype(BF), held, NT)
    is_held = dot(jnp.where(col == row, 1.0, 0.0).astype(BF), held, NT) > 0.5
    target = jnp.where(is_held, rank + 1.0, -2.0 * COMPACT).astype(jnp.int32)
    place = lax.broadcasted_iota(jnp.int32, (2 * slots, 2 * COMPACT), 1)
    for s in range(0, GROUP, 2):
        goal = jnp.concatenate([target[:, s : s + 1], target[:, s + 1 : s + 2] + COMPACT], axis=0)
        hot = jnp.where(place == goal, 1.0, 0.0).astype(BF)
        rows = dot(hot, got_ref[s : s + 2].reshape(2 * COMPACT, 2 * HEAD), NN)
        if mark:
            rows = jnp.concatenate(
                [jnp.where(goal > 0, rows[:, :HEAD], EMPTY), rows[:, HEAD:]], axis=1
            )
        out_ref[s : s + 2] = rows.reshape(2, slots, 2 * HEAD).astype(BF)


def spread(got, notes, mark):
    return pl.pallas_call(
        functools.partial(spread_kernel, mark),
        grid=(OWNERS // GROUP,),
        in_specs=[
            pl.BlockSpec((GROUP, COMPACT, 2 * HEAD), lambda p: (p, 0, 0)),
            pl.BlockSpec((GROUP, 2 * CELL, 2 * HEAD), lambda p: (p, 0, 0)),
        ],
        out_specs=pl.BlockSpec((GROUP, HEADS * CELL, 2 * HEAD), lambda p: (p, 0, 0)),
        out_shape=jax.ShapeDtypeStruct((OWNERS, HEADS * CELL, 2 * HEAD), BF),
        compiler_params=params("arbitrary"),
        cost_estimate=pl.CostEstimate(
            flops=2 * 2**30, bytes_accessed=8 * 2**20, transcendentals=0
        ),
        name="spread",
    )(got, notes)


def pack_kernel(mark, slot_ref, *refs):
    sources, out_ref = refs[:-1], refs[-1]
    place = lax.broadcasted_iota(jnp.int32, (SLOTS, TOK), 0)
    for n, source in enumerate(sources):
        parts = []
        for e in range(2):
            hot = jnp.where(place == slot_ref[0, e : e + 1, :], 1.0, 0.0)
            hot_low = hot.astype(BF)
            rows = dot(hot_low, source[:, e * HEAD : (e + 1) * HEAD], NN)
            if mark and n == 0:
                filled = dot(hot_low, jnp.ones((TOK, HEAD), BF), NN)
                rows = jnp.where(filled > 0.5, rows, EMPTY)
            parts.append(rows.reshape(OWNERS, CELL, HEAD))
        out_ref[:, :, n * HEAD : (n + 1) * HEAD] = jnp.concatenate(parts, axis=1).astype(BF)


def pack(slots, chunk, mark, *sources):
    pairs = HPC // 2
    width = HEAD * len(sources)
    return pl.pallas_call(
        functools.partial(pack_kernel, mark),
        grid=(pairs,),
        in_specs=[pl.BlockSpec((1, 2, TOK), lambda p: (chunk * pairs + p, 0, 0))]
        + [pl.BlockSpec((TOK, 2 * HEAD), lambda p: (0, chunk * pairs + p)) for _ in sources],
        out_specs=pl.BlockSpec((OWNERS, 2 * CELL, width), lambda p: (0, p, 0)),
        out_shape=jax.ShapeDtypeStruct((OWNERS, HPC * CELL, width), BF),
        compiler_params=params("arbitrary"),
        cost_estimate=pl.CostEstimate(
            flops=2 * HPC * SLOTS * TOK * width * 4, bytes_accessed=6 * 2**20, transcendentals=0
        ),
        name="pack",
    )(slots.reshape(HEADS // 2, 2, TOK), *sources)


def attention_kernel(kv_ref, gq_ref, out_ref, bias_ref):
    scale = 1.0 / math.sqrt(HEAD)
    to_exp2 = scale * math.log2(math.e)

    @pl.when(pl.program_id(0) == 0)
    def _():
        row = lax.broadcasted_iota(jnp.int32, (SLOTS, SLOTS), 0)
        col = lax.broadcasted_iota(jnp.int32, (SLOTS, SLOTS), 1)
        keep = (col <= row) & ((row % CELL) // 2 == (col % CELL) // 2)
        bias_ref[...] = jnp.where(keep, 0.0, -1e30)

    first = jnp.where(lax.broadcasted_iota(jnp.int32, (8, HEAD), 1) == 0, 1.0, 0.0).astype(BF)
    pairs = [ref[...].astype(F32) for ref in (kv_ref, gq_ref)]
    step = 256
    for e in range(2):
        kv, gq = (
            pair[:, e * CELL : (e + 1) * CELL, :].reshape(SLOTS, 2 * HEAD).astype(BF)
            for pair in pairs
        )
        k, v, g, q = kv[:, :HEAD], kv[:, HEAD:], gq[:, :HEAD], gq[:, HEAD:]
        key_bias = jnp.where(dot(first, k, NT)[0:1, :] > 0.5 * EMPTY, -1e30, 0.0)
        for i in range(SLOTS // step):
            here = slice(i * step, (i + 1) * step)
            n = (i + 1) * step
            score = dot(q[here], k[:n], NT) * to_exp2 + bias_ref[here, :n] + key_bias[:, :n]
            raised = jnp.exp2(score)
            total = jnp.sum(raised, axis=1, keepdims=True)
            weights = raised * (1.0 / jnp.where(total == 0.0, 1.0, total))
            attended = dot(weights.astype(BF), v[:n], NN)
            dweights = dot(g[here], v[:n], NT)
            delta = jnp.sum(g[here].astype(F32) * attended, axis=1, keepdims=True)
            dscores = (weights * (dweights - delta)).astype(BF)
            dquery = (dot(dscores, k[:n], NN) * scale).astype(BF)
            tiles = step // (2 * CELL)
            out_ref[0, i * tiles : (i + 1) * tiles, e] = dquery.reshape(tiles, 2 * CELL, HEAD)


def attention(kv, gq, first):
    return pl.pallas_call(
        attention_kernel,
        grid=(HPC // 2,),
        in_specs=[
            pl.BlockSpec((OWNERS, 2 * CELL, 2 * HEAD), lambda p: (0, first + p, 0)),
            pl.BlockSpec((OWNERS, 2 * CELL, 2 * HEAD), lambda p: (0, first + p, 0)),
        ],
        out_specs=pl.BlockSpec((1, OWNERS // 2, 2, 2 * CELL, HEAD), lambda p: (p, 0, 0, 0, 0)),
        out_shape=jax.ShapeDtypeStruct((HPC // 2, OWNERS // 2, 2, 2 * CELL, HEAD), BF),
        scratch_shapes=[pltpu.VMEM((SLOTS, SLOTS), F32)],
        compiler_params=params("arbitrary"),
        cost_estimate=pl.CostEstimate(
            flops=HPC * 8 * SLOTS * SLOTS * HEAD,
            bytes_accessed=5 * 2**20,
            transcendentals=HPC * SLOTS * SLOTS,
        ),
        name="attention",
    )(kv, gq)


def grad_kernel(where_ref, rows_ref, act_a, act_b, *refs):
    earlier_ref, out_ref, acc_ref = refs if len(refs) == 3 else (None, *refs)
    b = pl.program_id(0)
    head, core = where_ref[0], where_ref[1]
    features = acc_ref.shape[0]
    rows = rows_ref[...].reshape(OWNERS * 2 * CELL, HEAD)
    line = lax.broadcasted_iota(jnp.int32, (2 * HEADS, TOK), 0)
    place = lax.broadcasted_iota(jnp.int32, (OWNERS * 2 * CELL, TOK), 0)
    total = None
    for act_ref, side in ((act_a, core), (act_b, 1 - core)):
        slot = act_ref[0, features:, :].astype(F32)
        weight = jnp.where(line == head, 2.0 * CELL, jnp.where(line == HEADS + head, 1.0, 0.0))
        index = jnp.sum(slot * weight, axis=0, keepdims=True).astype(jnp.int32) + side * CELL
        hot = jnp.where(place == index, 1.0, 0.0).astype(BF)
        dquery = dot(rows, hot, ((0,), (0,))).astype(BF)
        term = dot(act_ref[0, :features, :], dquery, NT)
        total = term if total is None else total + term

    @pl.when(b == 0)
    def _():
        acc_ref[...] = total

    @pl.when(b > 0)
    def _():
        acc_ref[...] += total

    @pl.when(b == pl.num_programs(0) - 1)
    def _():
        if earlier_ref is None:
            out_ref[...] = acc_ref[...]
        else:
            both = [ref[...].reshape(-1, CELL, HEAD) for ref in (earlier_ref, acc_ref)]
            out_ref[...] = jnp.concatenate(both, axis=1).astype(BF)


def weight_grad(where, rows, acts, features, seqs, earlier):
    def act_spec():
        return pl.BlockSpec((1, features + CARRIED, TOK), lambda b, w: (b, 0, 0))

    in_specs = [
        pl.BlockSpec((OWNERS, 2 * CELL, HEAD), lambda b, w: (b, 0, 0)),
        act_spec(),
        act_spec(),
    ]
    if earlier is None:
        out = jax.ShapeDtypeStruct((features, HEAD), F32)
        out_spec = pl.BlockSpec((features, HEAD), lambda b, w: (0, 0))
        more = ()
    else:
        out = jax.ShapeDtypeStruct((features // CELL, 2 * CELL, HEAD), BF)
        out_spec = pl.BlockSpec((features // CELL, 2 * CELL, HEAD), lambda b, w: (0, 0, 0))
        in_specs.append(pl.BlockSpec((features, HEAD), lambda b, w: (0, 0)))
        more = (earlier,)
    return pl.pallas_call(
        grad_kernel,
        grid_spec=pltpu.PrefetchScalarGridSpec(
            num_scalar_prefetch=1,
            grid=(seqs,),
            in_specs=in_specs,
            out_specs=out_spec,
            scratch_shapes=[pltpu.VMEM((features, HEAD), F32)],
        ),
        out_shape=out,
        compiler_params=params("arbitrary"),
        cost_estimate=pl.CostEstimate(
            flops=4 * seqs * TOK * features * HEAD * 2,
            bytes_accessed=12 * 2**20,
            transcendentals=0,
        ),
        name="weight_grad",
    )(where, rows, *acts, *more)


def on_device(activations, w_query, all_keys, values, grad_out, cluster):
    tokens_here = activations[0]
    features = tokens_here.shape[1]
    seqs = lax.axis_size("dp")
    devices = seqs * OWNERS
    slots, held, row_of, over = slots_of(cluster[0])
    seq_send = functools.partial(
        lax.all_to_all, axis_name="seq", split_axis=0, concat_axis=0, tiled=True
    )
    all_send = functools.partial(
        lax.all_to_all, axis_name=("dp", "seq"), split_axis=0, concat_axis=0, tiled=True
    )
    keys, vals, grads = all_keys[0], values[0], grad_out[0]

    core = lax.axis_index("seq") % 2
    group = lax.axis_index("dp") * 2 + core
    flag = over
    for shift in range(1, seqs):
        ring = [(i, (i + shift) % seqs) for i in range(seqs)]
        flag = jnp.maximum(flag, lax.ppermute(over, "dp", ring))

    got_kv = seq_send(compact(slots, row_of, held, jnp.zeros((8, HEAD), F32), keys, vals))
    queries = jnp.dot(tokens_here, w_query, preferred_element_type=F32).astype(BF)
    send_gq = compact(slots, row_of, held, flag, grads, queries)
    carried = jnp.concatenate(
        [tokens_here.T, (slots // CELL).astype(BF), (slots % CELL).astype(BF)], axis=0
    )
    send_gq, got_kv, carried = lax.optimization_barrier((send_gq, got_kv, carried))
    got_gq = seq_send(send_gq)

    acts_mine = lax.all_gather(carried, "dp")
    acts = (acts_mine, lax.ppermute(acts_mine, "seq", [(i, i ^ 1) for i in range(OWNERS)]))

    def send_all_slots(state):
        def whole(mark, *sources):
            parts = [pack(slots, c, mark, *sources) for c in range(CHUNKS)]
            return seq_send(jnp.concatenate(parts, axis=1))

        return jnp.zeros_like(state[0]), whole(True, keys, vals), whole(False, grads, queries)

    too_many = jnp.max(got_gq[:, 0, HEAD]).astype(F32)
    spreads = (spread(got_kv, got_kv, True), spread(got_gq, got_kv, False))
    _, kv, gq = lax.while_loop(
        lambda state: state[0] > 0.5, send_all_slots, (too_many, *spreads)
    )
    part = None
    for c in range(CHUNKS):
        rows = attention(kv, gq, c * HPC // 2)
        back = all_send(rows.reshape(devices, 2 * CELL, HEAD))
        where = jnp.stack([c * HPC + group, core]).astype(jnp.int32)
        part = weight_grad(where, back, acts, features, seqs, part)
    terms = all_send(part)
    terms = terms.reshape(seqs, OWNERS // 2, 2, CHUNKS, features // devices, HEAD)
    out = jnp.sum(terms.astype(F32), axis=1)
    out = out.transpose(3, 2, 0, 1, 4)
    return out.reshape(features // devices, HEADS * HEAD)


def solution(mesh):
    placed = (
        P("dp", "seq", None),
        P(),
        P("dp", "seq", None),
        P("dp", "seq", None),
        P("dp", "seq", None),
        P("dp", "seq", None),
    )
    return jax.shard_map(
        on_device, mesh=mesh, in_specs=placed, out_specs=P(("dp", "seq"), None), check_vma=False
    )
```

```python
import functools
import math

import jax
import jax.numpy as jnp
from jax import lax
from jax.experimental import pallas as pl
from jax.experimental.pallas import tpu as pltpu
from jax.sharding import PartitionSpec as P

HEAD = 128
TOK = 256
OWNERS = 64
CELL = 8
SLOTS = OWNERS * CELL
HEADS = 16
CARRIED = 2 * HEADS
CHUNKS = 2
YS, ZS = 4, 8
HPC = HEADS // CHUNKS
COMPACT = 96
GROUP = 16
FILLS = 4
EMPTY = 128.0
VMEM = 48 * 1024 * 1024
BF = jnp.bfloat16
F32 = jnp.float32


def dot(a, b, dims):
    return lax.dot_general(a, b, (dims, ((), ())), preferred_element_type=F32)


NN = ((1,), (0,))
NT = ((1,), (1,))


def params(*semantics, vmem=VMEM):
    return pltpu.CompilerParams(vmem_limit_bytes=vmem, dimension_semantics=semantics or None)


def slot_kernel(col_ref, row_ref, out_ref, held_ref, row_of_ref, over_ref):
    earlier = lax.broadcasted_iota(jnp.int32, (TOK, TOK), 0) < lax.broadcasted_iota(
        jnp.int32, (TOK, TOK), 1
    )
    owners = lax.broadcasted_iota(jnp.int32, (OWNERS, TOK), 0)
    lanes = lax.broadcasted_iota(jnp.int32, (HEADS * CELL, TOK), 0)
    held = None
    for h in range(HEADS):
        row = row_ref[h : h + 1, :]
        same = (col_ref[:, h : h + 1] == row) & earlier
        rank = jnp.sum(jnp.where(same, 1, 0), axis=0, keepdims=True)
        owner = (row + 4 * h + row // OWNERS) % OWNERS
        cell = (row // OWNERS) * 2 + rank
        out_ref[h : h + 1, :] = owner * CELL + cell
        to_owner = jnp.where(owners == owner, 1.0, 0.0).astype(BF)
        to_lane = jnp.where(lanes == h * CELL + cell, 1.0, 0.0).astype(BF)
        term = dot(to_owner, to_lane, NT)
        held = term if held is None else held + term
    held_ref[...] = held
    before = lax.broadcasted_iota(jnp.int32, (HEADS * CELL, HEADS * CELL), 0) < (
        lax.broadcasted_iota(jnp.int32, (HEADS * CELL, HEADS * CELL), 1)
    )
    rank = dot(held.astype(BF), jnp.where(before, 1.0, 0.0).astype(BF), NN)
    row_of = jnp.where(held > 0.5, rank + 1.0, -1.0)
    row_of_ref[...] = row_of
    most = jnp.max(jnp.max(row_of, axis=0, keepdims=True), axis=1, keepdims=True)
    over_ref[...] = jnp.broadcast_to(jnp.where(most >= COMPACT, 1.0, 0.0), over_ref.shape)


def slots_of(assign):
    per_owner = jax.ShapeDtypeStruct((OWNERS, HEADS * CELL), F32)
    return pl.pallas_call(
        slot_kernel,
        out_shape=(
            jax.ShapeDtypeStruct((HEADS, TOK), jnp.int32),
            per_owner,
            per_owner,
            jax.ShapeDtypeStruct((8, HEAD), F32),
        ),
        compiler_params=params(),
        name="slots",
    )(assign, assign.T)


def compact_kernel(slot_ref, row_of_ref, held_ref, flag_ref, one_ref, two_ref, out_ref, buf_ref):
    p = pl.program_id(0)

    @pl.when(p < FILLS)
    def _():
        place = lax.broadcasted_iota(jnp.int32, (SLOTS, TOK), 0)
        for e in range(0, HEADS // FILLS, 2):
            parts = []
            for h in (e, e + 1):
                hot = jnp.where(place == slot_ref[0, h : h + 1, :], 1.0, 0.0).astype(BF)
                here = slice(h * HEAD, (h + 1) * HEAD)
                both = jnp.concatenate([one_ref[:, here], two_ref[:, here]], axis=1)
                parts.append(dot(hot, both, NN).reshape(OWNERS, CELL, 2 * HEAD))
            first = p * (HEADS // FILLS) * CELL + e * CELL
            at = pl.ds(pl.multiple_of(first, 2 * CELL), 2 * CELL)
            buf_ref[:, at, :] = jnp.concatenate(parts, axis=1).astype(BF)

    @pl.when(p >= FILLS)
    def _():
        first = pl.multiple_of((p - FILLS) * GROUP, GROUP)
        row_of = row_of_ref[pl.ds(first, GROUP), :]
        row_of = jnp.where(row_of < COMPACT, row_of, -2.0 * COMPACT).astype(jnp.int32)
        held = held_ref[pl.ds(first, GROUP), :]
        notes = jnp.concatenate([held, jnp.broadcast_to(flag_ref[0:1, :], held.shape)], axis=1)
        place = lax.broadcasted_iota(jnp.int32, (2 * COMPACT, 2 * HEAD), 0)
        line = lax.broadcasted_iota(jnp.int32, (2 * CELL, 2 * HEAD), 0)
        for d in range(0, GROUP, 2):
            target = jnp.concatenate([row_of[d : d + 1], row_of[d + 1 : d + 2] + COMPACT], axis=1)
            hot = jnp.where(place == target, 1.0, 0.0).astype(BF)
            rows = buf_ref[pl.ds(first + d, 2)].reshape(2 * HEADS * CELL, 2 * HEAD)
            block = dot(hot, rows, NN)
            for e in range(2):
                mine = block[e * COMPACT : (e + 1) * COMPACT]
                top = jnp.where(line == 0, notes[d + e : d + e + 1], mine[: 2 * CELL])
                out_ref[d + e] = jnp.concatenate([top, mine[2 * CELL :]], axis=0).astype(BF)


def compact(slots, row_of, held, flag, one, two):
    groups = OWNERS // GROUP
    share = HEADS // FILLS
    whole = pl.BlockSpec((OWNERS, HEADS * CELL), lambda p: (0, 0))
    source = pl.BlockSpec((TOK, share * HEAD), lambda p: (0, jnp.minimum(p, FILLS - 1)))
    return pl.pallas_call(
        compact_kernel,
        grid=(FILLS + groups,),
        in_specs=[
            pl.BlockSpec((1, share, TOK), lambda p: (jnp.minimum(p, FILLS - 1), 0, 0)),
            whole,
            whole,
            pl.BlockSpec((8, HEAD), lambda p: (0, 0)),
            source,
            source,
        ],
        out_specs=pl.BlockSpec(
            (GROUP, COMPACT, 2 * HEAD), lambda p: (jnp.maximum(p - FILLS, 0), 0, 0)
        ),
        out_shape=jax.ShapeDtypeStruct((OWNERS, COMPACT, 2 * HEAD), BF),
        scratch_shapes=[pltpu.VMEM((OWNERS, HEADS * CELL, 2 * HEAD), BF)],
        compiler_params=params("arbitrary", vmem=60 * 1024 * 1024),
        cost_estimate=pl.CostEstimate(
            flops=4 * 2**30, bytes_accessed=8 * 2**20, transcendentals=0
        ),
        name="compact",
    )(slots.reshape(FILLS, share, TOK), row_of, held, flag, one, two)


def spread_kernel(mark, got_ref, note_ref, out_ref):
    slots = HEADS * CELL
    row = lax.broadcasted_iota(jnp.int32, (slots, slots), 0)
    col = lax.broadcasted_iota(jnp.int32, (slots, slots), 1)
    held = note_ref[...].astype(F32)[:, 0, :HEAD].astype(BF)
    rank = dot(jnp.where(col < row, 1.0, 0.0).astype(BF), held, NT)
    is_held = dot(jnp.where(col == row, 1.0, 0.0).astype(BF), held, NT) > 0.5
    target = jnp.where(is_held, rank + 1.0, -2.0 * COMPACT).astype(jnp.int32)
    place = lax.broadcasted_iota(jnp.int32, (2 * slots, 2 * COMPACT), 1)
    for s in range(0, GROUP, 2):
        goal = jnp.concatenate([target[:, s : s + 1], target[:, s + 1 : s + 2] + COMPACT], axis=0)
        hot = jnp.where(place == goal, 1.0, 0.0).astype(BF)
        rows = dot(hot, got_ref[s : s + 2].reshape(2 * COMPACT, 2 * HEAD), NN)
        if mark:
            rows = jnp.concatenate(
                [jnp.where(goal > 0, rows[:, :HEAD], EMPTY), rows[:, HEAD:]], axis=1
            )
        out_ref[s : s + 2] = rows.reshape(2, slots, 2 * HEAD).astype(BF)


def spread(got, notes, mark):
    return pl.pallas_call(
        functools.partial(spread_kernel, mark),
        grid=(OWNERS // GROUP,),
        in_specs=[
            pl.BlockSpec((GROUP, COMPACT, 2 * HEAD), lambda p: (p, 0, 0)),
            pl.BlockSpec((GROUP, 2 * CELL, 2 * HEAD), lambda p: (p, 0, 0)),
        ],
        out_specs=pl.BlockSpec((GROUP, HEADS * CELL, 2 * HEAD), lambda p: (p, 0, 0)),
        out_shape=jax.ShapeDtypeStruct((OWNERS, HEADS * CELL, 2 * HEAD), BF),
        compiler_params=params("arbitrary"),
        cost_estimate=pl.CostEstimate(
            flops=2 * 2**30, bytes_accessed=8 * 2**20, transcendentals=0
        ),
        name="spread",
    )(got, notes)


def pack_kernel(mark, slot_ref, *refs):
    sources, out_ref = refs[:-1], refs[-1]
    place = lax.broadcasted_iota(jnp.int32, (SLOTS, TOK), 0)
    for n, source in enumerate(sources):
        parts = []
        for e in range(2):
            hot = jnp.where(place == slot_ref[0, e : e + 1, :], 1.0, 0.0)
            hot_low = hot.astype(BF)
            rows = dot(hot_low, source[:, e * HEAD : (e + 1) * HEAD], NN)
            if mark and n == 0:
                filled = dot(hot_low, jnp.ones((TOK, HEAD), BF), NN)
                rows = jnp.where(filled > 0.5, rows, EMPTY)
            parts.append(rows.reshape(OWNERS, CELL, HEAD))
        out_ref[:, :, n * HEAD : (n + 1) * HEAD] = jnp.concatenate(parts, axis=1).astype(BF)


def pack(slots, chunk, mark, *sources):
    pairs = HPC // 2
    width = HEAD * len(sources)
    return pl.pallas_call(
        functools.partial(pack_kernel, mark),
        grid=(pairs,),
        in_specs=[pl.BlockSpec((1, 2, TOK), lambda p: (chunk * pairs + p, 0, 0))]
        + [pl.BlockSpec((TOK, 2 * HEAD), lambda p: (0, chunk * pairs + p)) for _ in sources],
        out_specs=pl.BlockSpec((OWNERS, 2 * CELL, width), lambda p: (0, p, 0)),
        out_shape=jax.ShapeDtypeStruct((OWNERS, HPC * CELL, width), BF),
        compiler_params=params("arbitrary"),
        cost_estimate=pl.CostEstimate(
            flops=2 * HPC * SLOTS * TOK * width * 4, bytes_accessed=6 * 2**20, transcendentals=0
        ),
        name="pack",
    )(slots.reshape(HEADS // 2, 2, TOK), *sources)


def attention_kernel(kv_ref, gq_ref, out_ref, bias_ref):
    scale = 1.0 / math.sqrt(HEAD)
    to_exp2 = scale * math.log2(math.e)

    @pl.when(pl.program_id(0) == 0)
    def _():
        row = lax.broadcasted_iota(jnp.int32, (SLOTS, SLOTS), 0)
        col = lax.broadcasted_iota(jnp.int32, (SLOTS, SLOTS), 1)
        keep = (col <= row) & ((row % CELL) // 2 == (col % CELL) // 2)
        bias_ref[...] = jnp.where(keep, 0.0, -1e30)

    first = jnp.where(lax.broadcasted_iota(jnp.int32, (8, HEAD), 1) == 0, 1.0, 0.0).astype(BF)
    pairs = [ref[...].astype(F32) for ref in (kv_ref, gq_ref)]
    step = 256
    for e in range(2):
        kv, gq = (
            pair[:, e * CELL : (e + 1) * CELL, :].reshape(SLOTS, 2 * HEAD).astype(BF)
            for pair in pairs
        )
        k, v, g, q = kv[:, :HEAD], kv[:, HEAD:], gq[:, :HEAD], gq[:, HEAD:]
        key_bias = jnp.where(dot(first, k, NT)[0:1, :] > 0.5 * EMPTY, -1e30, 0.0)
        for i in range(SLOTS // step):
            here = slice(i * step, (i + 1) * step)
            n = (i + 1) * step
            score = dot(q[here], k[:n], NT) * to_exp2 + bias_ref[here, :n] + key_bias[:, :n]
            raised = jnp.exp2(score)
            total = jnp.sum(raised, axis=1, keepdims=True)
            weights = raised * (1.0 / jnp.where(total == 0.0, 1.0, total))
            attended = dot(weights.astype(BF), v[:n], NN)
            dweights = dot(g[here], v[:n], NT)
            delta = jnp.sum(g[here].astype(F32) * attended, axis=1, keepdims=True)
            dscores = (weights * (dweights - delta)).astype(BF)
            dquery = (dot(dscores, k[:n], NN) * scale).astype(BF)
            tiles = step // (2 * CELL)
            out_ref[0, i * tiles : (i + 1) * tiles, e] = dquery.reshape(tiles, 2 * CELL, HEAD)


def attention(kv, gq, first):
    return pl.pallas_call(
        attention_kernel,
        grid=(HPC // 2,),
        in_specs=[
            pl.BlockSpec((OWNERS, 2 * CELL, 2 * HEAD), lambda p: (0, first + p, 0)),
            pl.BlockSpec((OWNERS, 2 * CELL, 2 * HEAD), lambda p: (0, first + p, 0)),
        ],
        out_specs=pl.BlockSpec((1, OWNERS // 2, 2, 2 * CELL, HEAD), lambda p: (p, 0, 0, 0, 0)),
        out_shape=jax.ShapeDtypeStruct((HPC // 2, OWNERS // 2, 2, 2 * CELL, HEAD), BF),
        scratch_shapes=[pltpu.VMEM((SLOTS, SLOTS), F32)],
        compiler_params=params("arbitrary"),
        cost_estimate=pl.CostEstimate(
            flops=HPC * 8 * SLOTS * SLOTS * HEAD,
            bytes_accessed=5 * 2**20,
            transcendentals=HPC * SLOTS * SLOTS,
        ),
        name="attention",
    )(kv, gq)


def grad_kernel(where_ref, rows_ref, act_a, act_b, out_ref, acc_ref):
    b = pl.program_id(0)
    head, core = where_ref[0], where_ref[1]
    features = acc_ref.shape[0]
    rows = rows_ref[...].reshape(OWNERS * 2 * CELL, HEAD)
    line = lax.broadcasted_iota(jnp.int32, (2 * HEADS, TOK), 0)
    place = lax.broadcasted_iota(jnp.int32, (OWNERS * 2 * CELL, TOK), 0)
    total = None
    for act_ref, side in ((act_a, core), (act_b, 1 - core)):
        slot = act_ref[0, features:, :].astype(F32)
        weight = jnp.where(line == head, 2.0 * CELL, jnp.where(line == HEADS + head, 1.0, 0.0))
        index = jnp.sum(slot * weight, axis=0, keepdims=True).astype(jnp.int32) + side * CELL
        hot = jnp.where(place == index, 1.0, 0.0).astype(BF)
        dquery = dot(rows, hot, ((0,), (0,))).astype(BF)
        term = dot(act_ref[0, :features, :], dquery, NT)
        total = term if total is None else total + term

    @pl.when(b == 0)
    def _():
        acc_ref[...] = total

    @pl.when(b > 0)
    def _():
        acc_ref[...] += total

    @pl.when(b == pl.num_programs(0) - 1)
    def _():
        ys, zs, seqs, pair = out_ref.shape[:4]
        for y in range(ys):
            for z in range(zs):
                for d in range(seqs):
                    at = ((d * ys + y) * zs + z) * pair
                    out_ref[y, z, d] = acc_ref[at : at + pair, :].astype(BF)


def weight_grad(where, rows, acts, features, seqs):
    def act_spec():
        return pl.BlockSpec((1, features + CARRIED, TOK), lambda b, w: (b, 0, 0))

    out = (YS, ZS, seqs, features // (YS * ZS * seqs), HEAD)
    return pl.pallas_call(
        grad_kernel,
        grid_spec=pltpu.PrefetchScalarGridSpec(
            num_scalar_prefetch=1,
            grid=(seqs,),
            in_specs=[
                pl.BlockSpec((OWNERS, 2 * CELL, HEAD), lambda b, w: (b, 0, 0)),
                act_spec(),
                act_spec(),
            ],
            out_specs=pl.BlockSpec(out, lambda b, w: (0, 0, 0, 0, 0)),
            scratch_shapes=[pltpu.VMEM((features, HEAD), F32)],
        ),
        out_shape=jax.ShapeDtypeStruct(out, BF),
        compiler_params=params("arbitrary", vmem=60 * 1024 * 1024),
        cost_estimate=pl.CostEstimate(
            flops=4 * seqs * TOK * features * HEAD * 2,
            bytes_accessed=12 * 2**20,
            transcendentals=0,
        ),
        name="weight_grad",
    )(where, rows, *acts)


def on_device(activations, w_query, all_keys, values, grad_out, cluster):
    tokens_here = activations[0]
    features = tokens_here.shape[1]
    seqs = lax.axis_size("dp")
    devices = seqs * OWNERS
    slots, held, row_of, over = slots_of(cluster[0])
    seq_send = functools.partial(
        lax.all_to_all, axis_name="seq", split_axis=0, concat_axis=0, tiled=True
    )
    all_send = functools.partial(
        lax.all_to_all, axis_name=("dp", "seq"), split_axis=0, concat_axis=0, tiled=True
    )
    keys, vals, grads = all_keys[0], values[0], grad_out[0]

    core = lax.axis_index("seq") % 2
    group = lax.axis_index("dp") * 2 + core
    flag = over
    for shift in range(1, seqs):
        ring = [(i, (i + shift) % seqs) for i in range(seqs)]
        flag = jnp.maximum(flag, lax.ppermute(over, "dp", ring))

    got_kv = seq_send(compact(slots, row_of, held, jnp.zeros((8, HEAD), F32), keys, vals))
    queries = jnp.dot(tokens_here, w_query, preferred_element_type=F32).astype(BF)
    send_gq = compact(slots, row_of, held, flag, grads, queries)
    carried = jnp.concatenate(
        [tokens_here.T, (slots // CELL).astype(BF), (slots % CELL).astype(BF)], axis=0
    )
    send_gq, got_kv, carried = lax.optimization_barrier((send_gq, got_kv, carried))
    got_gq = seq_send(send_gq)

    acts_mine = lax.all_gather(carried, "dp")
    acts = (acts_mine, lax.ppermute(acts_mine, "seq", [(i, i ^ 1) for i in range(OWNERS)]))

    def send_all_slots(state):
        def whole(mark, *sources):
            parts = [pack(slots, c, mark, *sources) for c in range(CHUNKS)]
            return seq_send(jnp.concatenate(parts, axis=1))

        return jnp.zeros_like(state[0]), whole(True, keys, vals), whole(False, grads, queries)

    too_many = jnp.max(got_gq[:, 0, HEAD]).astype(F32)
    spreads = (spread(got_kv, got_kv, True), spread(got_gq, got_kv, False))
    _, kv, gq = lax.while_loop(
        lambda state: state[0] > 0.5, send_all_slots, (too_many, *spreads)
    )
    rows = [attention(kv, gq, c * HPC // 2).reshape(devices, 2 * CELL, HEAD) for c in range(CHUNKS)]
    back = all_send(rows[0])
    rows[1], back = lax.optimization_barrier((rows[1], back))
    back_next = all_send(rows[1])
    wheres = [jnp.stack([c * HPC + group, core]).astype(jnp.int32) for c in range(CHUNKS)]

    def place(y, z, side):
        return (y * ZS + z) * 2 + side

    part = weight_grad(wheres[0], back, acts, features, seqs)
    my_y = lax.axis_index("seq") // (2 * ZS)
    first = lax.dynamic_index_in_dim(part, my_y, 0, False).astype(F32)
    for shift in range(1, YS):
        ring = [
            (place(y, z, side), place((y + shift) % YS, z, side))
            for y in range(YS)
            for z in range(ZS)
            for side in range(2)
        ]
        block = lax.dynamic_index_in_dim(part, (my_y + shift) % YS, 0, False)
        first = first + lax.ppermute(block, "seq", ring).astype(F32)
    back_next, first = lax.optimization_barrier((back_next, first))
    part = weight_grad(wheres[1], back_next, acts, features, seqs)
    along_y = [[place(y, z, side) for y in range(YS)] for z in range(ZS) for side in range(2)]
    second = jnp.sum(seq_send(part, axis_index_groups=along_y).astype(F32), axis=0)
    along_z = [[place(y, z, side) for z in range(ZS)] for y in range(YS) for side in range(2)]
    both = jnp.concatenate([first, second], axis=2).astype(BF)
    both = jnp.sum(seq_send(both, axis_index_groups=along_z).astype(F32), axis=0)
    both = both.reshape(seqs, CHUNKS, 2, features // devices, HEAD).transpose(0, 2, 1, 3, 4)
    both = both.reshape(2 * seqs, CHUNKS, features // devices, HEAD)
    around = [
        [d * OWNERS + p * 2 + side for d in range(seqs) for side in range(2)]
        for p in range(OWNERS // 2)
    ]
    out = all_send(both, axis_index_groups=around)
    return out.transpose(2, 1, 0, 3).reshape(features // devices, HEADS * HEAD)


def solution(mesh):
    placed = (
        P("dp", "seq", None),
        P(),
        P("dp", "seq", None),
        P("dp", "seq", None),
        P("dp", "seq", None),
        P("dp", "seq", None),
    )
    return jax.shard_map(
        on_device, mesh=mesh, in_specs=placed, out_specs=P(("dp", "seq"), None), check_vma=False
    )
```

```python
import functools
import math

import jax
import jax.numpy as jnp
from jax import lax
from jax.experimental import pallas as pl
from jax.experimental.pallas import tpu as pltpu
from jax.sharding import PartitionSpec as P

HEAD = 128
TOK = 256
OWNERS = 64
CELL = 8
SLOTS = OWNERS * CELL
HEADS = 16
CARRIED = 2 * HEADS
CHUNKS = 2
HPC = HEADS // CHUNKS
COMPACT = 96
GROUP = 32
FILLS = 2
EMPTY = 128.0
VMEM = 48 * 1024 * 1024
BF = jnp.bfloat16
F32 = jnp.float32


def dot(a, b, dims):
    return lax.dot_general(a, b, (dims, ((), ())), preferred_element_type=F32)


NN = ((1,), (0,))
NT = ((1,), (1,))


def params(*semantics, vmem=VMEM):
    return pltpu.CompilerParams(vmem_limit_bytes=vmem, dimension_semantics=semantics or None)


def slot_kernel(col_ref, row_ref, out_ref, held_ref, row_of_ref, over_ref):
    earlier = lax.broadcasted_iota(jnp.int32, (TOK, TOK), 0) < lax.broadcasted_iota(
        jnp.int32, (TOK, TOK), 1
    )
    owners = lax.broadcasted_iota(jnp.int32, (OWNERS, TOK), 0)
    lanes = lax.broadcasted_iota(jnp.int32, (HEADS * CELL, TOK), 0)
    held = None
    for h in range(HEADS):
        row = row_ref[h : h + 1, :]
        same = (col_ref[:, h : h + 1] == row) & earlier
        rank = jnp.sum(jnp.where(same, 1, 0), axis=0, keepdims=True)
        owner = (row + 4 * h + row // OWNERS) % OWNERS
        cell = (row // OWNERS) * 2 + rank
        out_ref[h : h + 1, :] = owner * CELL + cell
        to_owner = jnp.where(owners == owner, 1.0, 0.0).astype(BF)
        to_lane = jnp.where(lanes == h * CELL + cell, 1.0, 0.0).astype(BF)
        term = dot(to_owner, to_lane, NT)
        held = term if held is None else held + term
    held_ref[...] = held
    before = lax.broadcasted_iota(jnp.int32, (HEADS * CELL, HEADS * CELL), 0) < (
        lax.broadcasted_iota(jnp.int32, (HEADS * CELL, HEADS * CELL), 1)
    )
    rank = dot(held.astype(BF), jnp.where(before, 1.0, 0.0).astype(BF), NN)
    row_of = jnp.where(held > 0.5, rank + 1.0, -1.0)
    row_of_ref[...] = row_of
    most = jnp.max(jnp.max(row_of, axis=0, keepdims=True), axis=1, keepdims=True)
    over_ref[...] = jnp.broadcast_to(jnp.where(most >= COMPACT, 1.0, 0.0), over_ref.shape)


def slots_of(assign):
    per_owner = jax.ShapeDtypeStruct((OWNERS, HEADS * CELL), F32)
    return pl.pallas_call(
        slot_kernel,
        out_shape=(
            jax.ShapeDtypeStruct((HEADS, TOK), jnp.int32),
            per_owner,
            per_owner,
            jax.ShapeDtypeStruct((8, HEAD), F32),
        ),
        compiler_params=params(),
        name="slots",
    )(assign, assign.T)


def compact_kernel(slot_ref, row_of_ref, held_ref, flag_ref, one_ref, two_ref, out_ref, buf_ref):
    p = pl.program_id(0)

    @pl.when(p < FILLS)
    def _():
        place = lax.broadcasted_iota(jnp.int32, (SLOTS, TOK), 0)
        for e in range(0, HEADS // FILLS, 2):
            parts = []
            for h in (e, e + 1):
                hot = jnp.where(place == slot_ref[0, h : h + 1, :], 1.0, 0.0).astype(BF)
                here = slice(h * HEAD, (h + 1) * HEAD)
                both = jnp.concatenate([one_ref[:, here], two_ref[:, here]], axis=1)
                parts.append(dot(hot, both, NN).reshape(OWNERS, CELL, 2 * HEAD))
            first = p * (HEADS // FILLS) * CELL + e * CELL
            at = pl.ds(pl.multiple_of(first, 2 * CELL), 2 * CELL)
            buf_ref[:, at, :] = jnp.concatenate(parts, axis=1).astype(BF)

    @pl.when(p >= FILLS)
    def _():
        first = pl.multiple_of((p - FILLS) * GROUP, GROUP)
        row_of = row_of_ref[pl.ds(first, GROUP), :]
        row_of = jnp.where(row_of < COMPACT, row_of, -2.0 * COMPACT).astype(jnp.int32)
        held = held_ref[pl.ds(first, GROUP), :]
        notes = jnp.concatenate([held, jnp.broadcast_to(flag_ref[0:1, :], held.shape)], axis=1)
        place = lax.broadcasted_iota(jnp.int32, (2 * COMPACT, 2 * HEAD), 0)
        line = lax.broadcasted_iota(jnp.int32, (2 * CELL, 2 * HEAD), 0)
        for d in range(0, GROUP, 2):
            target = jnp.concatenate([row_of[d : d + 1], row_of[d + 1 : d + 2] + COMPACT], axis=1)
            hot = jnp.where(place == target, 1.0, 0.0).astype(BF)
            rows = buf_ref[pl.ds(first + d, 2)].reshape(2 * HEADS * CELL, 2 * HEAD)
            block = dot(hot, rows, NN)
            for e in range(2):
                mine = block[e * COMPACT : (e + 1) * COMPACT]
                top = jnp.where(line == 0, notes[d + e : d + e + 1], mine[: 2 * CELL])
                out_ref[d + e] = jnp.concatenate([top, mine[2 * CELL :]], axis=0).astype(BF)


def compact(slots, row_of, held, flag, one, two):
    groups = OWNERS // GROUP
    share = HEADS // FILLS
    whole = pl.BlockSpec((OWNERS, HEADS * CELL), lambda p: (0, 0))
    source = pl.BlockSpec((TOK, share * HEAD), lambda p: (0, jnp.minimum(p, FILLS - 1)))
    return pl.pallas_call(
        compact_kernel,
        grid=(FILLS + groups,),
        in_specs=[
            pl.BlockSpec((1, share, TOK), lambda p: (jnp.minimum(p, FILLS - 1), 0, 0)),
            whole,
            whole,
            pl.BlockSpec((8, HEAD), lambda p: (0, 0)),
            source,
            source,
        ],
        out_specs=pl.BlockSpec(
            (GROUP, COMPACT, 2 * HEAD), lambda p: (jnp.maximum(p - FILLS, 0), 0, 0)
        ),
        out_shape=jax.ShapeDtypeStruct((OWNERS, COMPACT, 2 * HEAD), BF),
        scratch_shapes=[pltpu.VMEM((OWNERS, HEADS * CELL, 2 * HEAD), BF)],
        compiler_params=params("arbitrary", vmem=60 * 1024 * 1024),
        cost_estimate=pl.CostEstimate(
            flops=4 * 2**30, bytes_accessed=8 * 2**20, transcendentals=0
        ),
        name="compact",
    )(slots.reshape(FILLS, share, TOK), row_of, held, flag, one, two)


def spread_kernel(mark, got_ref, note_ref, out_ref, flag_ref):
    notes = got_ref[:, : 2 * CELL, HEAD:].astype(F32)[:, 0, :]
    flag = jnp.broadcast_to(jnp.max(notes, axis=0, keepdims=True), flag_ref.shape)

    @pl.when(pl.program_id(0) == 0)
    def _():
        flag_ref[...] = flag

    @pl.when(pl.program_id(0) > 0)
    def _():
        flag_ref[...] = jnp.maximum(flag_ref[...], flag)

    slots = HEADS * CELL
    row = lax.broadcasted_iota(jnp.int32, (slots, slots), 0)
    col = lax.broadcasted_iota(jnp.int32, (slots, slots), 1)
    held = note_ref[...].astype(F32)[:, 0, :HEAD].astype(BF)
    rank = dot(jnp.where(col < row, 1.0, 0.0).astype(BF), held, NT)
    is_held = dot(jnp.where(col == row, 1.0, 0.0).astype(BF), held, NT) > 0.5
    target = jnp.where(is_held, rank + 1.0, -2.0 * COMPACT).astype(jnp.int32)
    place = lax.broadcasted_iota(jnp.int32, (2 * slots, 2 * COMPACT), 1)
    for s in range(0, GROUP, 2):
        goal = jnp.concatenate([target[:, s : s + 1], target[:, s + 1 : s + 2] + COMPACT], axis=0)
        hot = jnp.where(place == goal, 1.0, 0.0).astype(BF)
        rows = dot(hot, got_ref[s : s + 2].reshape(2 * COMPACT, 2 * HEAD), NN)
        if mark:
            rows = jnp.concatenate(
                [jnp.where(goal > 0, rows[:, :HEAD], EMPTY), rows[:, HEAD:]], axis=1
            )
        out_ref[s : s + 2] = rows.reshape(2, slots, 2 * HEAD).astype(BF)


def spread(got, notes, mark):
    return pl.pallas_call(
        functools.partial(spread_kernel, mark),
        grid=(OWNERS // GROUP,),
        in_specs=[
            pl.BlockSpec((GROUP, COMPACT, 2 * HEAD), lambda p: (p, 0, 0)),
            pl.BlockSpec((GROUP, 2 * CELL, 2 * HEAD), lambda p: (p, 0, 0)),
        ],
        out_specs=(
            pl.BlockSpec((GROUP, HEADS * CELL, 2 * HEAD), lambda p: (p, 0, 0)),
            pl.BlockSpec((8, HEAD), lambda p: (0, 0)),
        ),
        out_shape=(
            jax.ShapeDtypeStruct((OWNERS, HEADS * CELL, 2 * HEAD), BF),
            jax.ShapeDtypeStruct((8, HEAD), F32),
        ),
        compiler_params=params("arbitrary"),
        cost_estimate=pl.CostEstimate(
            flops=2 * 2**30, bytes_accessed=8 * 2**20, transcendentals=0
        ),
        name="spread",
    )(got, notes)


def pack_kernel(mark, slot_ref, *refs):
    sources, out_ref = refs[:-1], refs[-1]
    place = lax.broadcasted_iota(jnp.int32, (SLOTS, TOK), 0)
    for n, source in enumerate(sources):
        parts = []
        for e in range(2):
            hot = jnp.where(place == slot_ref[0, e : e + 1, :], 1.0, 0.0)
            hot_low = hot.astype(BF)
            rows = dot(hot_low, source[:, e * HEAD : (e + 1) * HEAD], NN)
            if mark and n == 0:
                filled = dot(hot_low, jnp.ones((TOK, HEAD), BF), NN)
                rows = jnp.where(filled > 0.5, rows, EMPTY)
            parts.append(rows.reshape(OWNERS, CELL, HEAD))
        out_ref[:, :, n * HEAD : (n + 1) * HEAD] = jnp.concatenate(parts, axis=1).astype(BF)


def pack(slots, chunk, mark, *sources):
    pairs = HPC // 2
    width = HEAD * len(sources)
    return pl.pallas_call(
        functools.partial(pack_kernel, mark),
        grid=(pairs,),
        in_specs=[pl.BlockSpec((1, 2, TOK), lambda p: (chunk * pairs + p, 0, 0))]
        + [pl.BlockSpec((TOK, 2 * HEAD), lambda p: (0, chunk * pairs + p)) for _ in sources],
        out_specs=pl.BlockSpec((OWNERS, 2 * CELL, width), lambda p: (0, p, 0)),
        out_shape=jax.ShapeDtypeStruct((OWNERS, HPC * CELL, width), BF),
        compiler_params=params("arbitrary"),
        cost_estimate=pl.CostEstimate(
            flops=2 * HPC * SLOTS * TOK * width * 4, bytes_accessed=6 * 2**20, transcendentals=0
        ),
        name="pack",
    )(slots.reshape(HEADS // 2, 2, TOK), *sources)


def attention_kernel(kv_ref, gq_ref, out_ref, bias_ref):
    scale = 1.0 / math.sqrt(HEAD)
    to_exp2 = scale * math.log2(math.e)

    @pl.when(pl.program_id(0) == 0)
    def _():
        row = lax.broadcasted_iota(jnp.int32, (SLOTS, SLOTS), 0)
        col = lax.broadcasted_iota(jnp.int32, (SLOTS, SLOTS), 1)
        keep = (col <= row) & ((row % CELL) // 2 == (col % CELL) // 2)
        bias_ref[...] = jnp.where(keep, 0.0, -1e30)

    first = jnp.where(lax.broadcasted_iota(jnp.int32, (8, HEAD), 1) == 0, 1.0, 0.0).astype(BF)
    def halves(ref):
        pair = ref[...].astype(F32)
        heads = [pair[:, e * CELL : (e + 1) * CELL, :].reshape(SLOTS, 2 * HEAD) for e in range(2)]
        return [x[:, n * HEAD : (n + 1) * HEAD].astype(BF) for n in range(2) for x in heads]

    both = range(2)
    k, v = (lambda x: (x[:2], x[2:]))(halves(kv_ref))
    g, q = (lambda x: (x[:2], x[2:]))(halves(gq_ref))
    key_bias = [
        jnp.where(dot(first, k[e], NT)[0:1, :] > 0.5 * EMPTY, -1e30, 0.0) for e in both
    ]
    scores = [dot(q[e], k[e], NT) for e in both]
    dweights = [dot(g[e], v[e], NT) for e in both]
    raised = [jnp.exp2(scores[e] * to_exp2 + bias_ref[...] + key_bias[e]) for e in both]
    totals = [jnp.sum(raised[e], axis=1, keepdims=True) for e in both]
    weights = [raised[e] * (1.0 / jnp.where(totals[e] == 0.0, 1.0, totals[e])) for e in both]
    attended = [dot(weights[e].astype(BF), v[e], NN) for e in both]
    delta = [jnp.sum(g[e].astype(F32) * attended[e], axis=1, keepdims=True) for e in both]
    dscores = [(weights[e] * (dweights[e] - delta[e])).astype(BF) for e in both]
    for e in both:
        dquery = (dot(dscores[e], k[e], NN) * scale).astype(BF)
        out_ref[0, :, e] = dquery.reshape(OWNERS // 2, 2 * CELL, HEAD)


def attention(kv, gq, first):
    return pl.pallas_call(
        attention_kernel,
        grid=(HPC // 2,),
        in_specs=[
            pl.BlockSpec((OWNERS, 2 * CELL, 2 * HEAD), lambda p: (0, first + p, 0)),
            pl.BlockSpec((OWNERS, 2 * CELL, 2 * HEAD), lambda p: (0, first + p, 0)),
        ],
        out_specs=pl.BlockSpec((1, OWNERS // 2, 2, 2 * CELL, HEAD), lambda p: (p, 0, 0, 0, 0)),
        out_shape=jax.ShapeDtypeStruct((HPC // 2, OWNERS // 2, 2, 2 * CELL, HEAD), BF),
        scratch_shapes=[pltpu.VMEM((SLOTS, SLOTS), F32)],
        compiler_params=params("arbitrary"),
        cost_estimate=pl.CostEstimate(
            flops=HPC * 8 * SLOTS * SLOTS * HEAD,
            bytes_accessed=5 * 2**20,
            transcendentals=HPC * SLOTS * SLOTS,
        ),
        name="attention",
    )(kv, gq)


def grad_kernel(where_ref, rows_ref, act_a, act_b, *refs):
    earlier_ref, out_ref, acc_ref = refs if len(refs) == 3 else (None, *refs)
    b = pl.program_id(0)
    head, core = where_ref[0], where_ref[1]
    features = acc_ref.shape[0]
    rows = rows_ref[...].astype(F32)
    low, high = (rows[:, e * CELL : (e + 1) * CELL].reshape(SLOTS, HEAD) for e in range(2))
    mine = jnp.where(core == 0, low, high).astype(BF)
    other = jnp.where(core == 0, high, low).astype(BF)
    line = lax.broadcasted_iota(jnp.int32, (2 * HEADS, TOK), 0)
    place = lax.broadcasted_iota(jnp.int32, (SLOTS, TOK), 0)
    total = None
    for act_ref, rows in ((act_a, mine), (act_b, other)):
        slot = act_ref[0, features:, :].astype(F32)
        weight = jnp.where(line == head, 1.0 * CELL, jnp.where(line == HEADS + head, 1.0, 0.0))
        index = jnp.sum(slot * weight, axis=0, keepdims=True).astype(jnp.int32)
        hot = jnp.where(place == index, 1.0, 0.0).astype(BF)
        dquery = dot(rows, hot, ((0,), (0,))).astype(BF)
        term = dot(act_ref[0, :features, :], dquery, NT)
        total = term if total is None else total + term

    @pl.when(b == 0)
    def _():
        acc_ref[...] = total

    @pl.when(b > 0)
    def _():
        acc_ref[...] += total

    @pl.when(b == pl.num_programs(0) - 1)
    def _():
        if earlier_ref is None:
            out_ref[...] = acc_ref[...]
        else:
            both = [ref[...].reshape(-1, CELL, HEAD) for ref in (earlier_ref, acc_ref)]
            out_ref[...] = jnp.concatenate(both, axis=1).astype(BF)


def weight_grad(where, rows, acts, features, seqs, earlier):
    def act_spec():
        return pl.BlockSpec((1, features + CARRIED, TOK), lambda b, w: (b, 0, 0))

    in_specs = [
        pl.BlockSpec((OWNERS, 2 * CELL, HEAD), lambda b, w: (b, 0, 0)),
        act_spec(),
        act_spec(),
    ]
    if earlier is None:
        out = jax.ShapeDtypeStruct((features, HEAD), F32)
        out_spec = pl.BlockSpec((features, HEAD), lambda b, w: (0, 0))
        more = ()
    else:
        out = jax.ShapeDtypeStruct((features // CELL, 2 * CELL, HEAD), BF)
        out_spec = pl.BlockSpec((features // CELL, 2 * CELL, HEAD), lambda b, w: (0, 0, 0))
        in_specs.append(pl.BlockSpec((features, HEAD), lambda b, w: (0, 0)))
        more = (earlier,)
    return pl.pallas_call(
        grad_kernel,
        grid_spec=pltpu.PrefetchScalarGridSpec(
            num_scalar_prefetch=1,
            grid=(seqs,),
            in_specs=in_specs,
            out_specs=out_spec,
            scratch_shapes=[pltpu.VMEM((features, HEAD), F32)],
        ),
        out_shape=out,
        compiler_params=params("arbitrary"),
        cost_estimate=pl.CostEstimate(
            flops=4 * seqs * TOK * features * HEAD * 2,
            bytes_accessed=12 * 2**20,
            transcendentals=0,
        ),
        name="weight_grad",
    )(where, rows, *acts, *more)


def on_device(activations, w_query, all_keys, values, grad_out, cluster):
    tokens_here = activations[0]
    features = tokens_here.shape[1]
    seqs = lax.axis_size("dp")
    devices = seqs * OWNERS
    slots, held, row_of, over = slots_of(cluster[0])
    seq_send = functools.partial(
        lax.all_to_all, axis_name="seq", split_axis=0, concat_axis=0, tiled=True
    )
    all_send = functools.partial(
        lax.all_to_all, axis_name=("dp", "seq"), split_axis=0, concat_axis=0, tiled=True
    )
    keys, vals, grads = all_keys[0], values[0], grad_out[0]

    core = lax.axis_index("seq") % 2
    group = lax.axis_index("dp") * 2 + core
    flag = over
    for shift in range(1, seqs):
        ring = [(i, (i + shift) % seqs) for i in range(seqs)]
        flag = jnp.maximum(flag, lax.ppermute(over, "dp", ring))

    got_kv = seq_send(compact(slots, row_of, held, jnp.zeros((8, HEAD), F32), keys, vals))
    queries = jnp.dot(tokens_here, w_query, preferred_element_type=F32).astype(BF)
    send_gq = compact(slots, row_of, held, flag, grads, queries)
    carried = jnp.concatenate(
        [tokens_here.T, (slots // CELL).astype(BF), (slots % CELL).astype(BF)], axis=0
    )
    send_gq, got_kv, carried = lax.optimization_barrier((send_gq, got_kv, carried))
    got_gq = seq_send(send_gq)

    acts_mine = lax.all_gather(carried, "dp")
    acts = (acts_mine, lax.ppermute(acts_mine, "seq", [(i, i ^ 1) for i in range(OWNERS)]))

    def send_all_slots(state):
        def whole(mark, *sources):
            parts = [pack(slots, c, mark, *sources) for c in range(CHUNKS)]
            return seq_send(jnp.concatenate(parts, axis=1))

        return jnp.zeros_like(state[0]), whole(True, keys, vals), whole(False, grads, queries)

    kv, _ = spread(got_kv, got_kv, True)
    gq, flags = spread(got_gq, got_kv, False)
    _, kv, gq = lax.while_loop(
        lambda state: state[0] > 0.5, send_all_slots, (flags[0, 0], kv, gq)
    )
    part = None
    for c in range(CHUNKS):
        rows = attention(kv, gq, c * HPC // 2)
        back = all_send(rows.reshape(devices, 2 * CELL, HEAD))
        where = jnp.stack([c * HPC + group, core]).astype(jnp.int32)
        part = weight_grad(where, back, acts, features, seqs, part)
    terms = all_send(part)
    terms = terms.reshape(seqs, OWNERS // 2, 2, CHUNKS, features // devices, HEAD)
    out = jnp.sum(terms.astype(F32), axis=1)
    out = out.transpose(3, 2, 0, 1, 4)
    return out.reshape(features // devices, HEADS * HEAD)


def solution(mesh):
    placed = (
        P("dp", "seq", None),
        P(),
        P("dp", "seq", None),
        P("dp", "seq", None),
        P("dp", "seq", None),
        P("dp", "seq", None),
    )
    return jax.shard_map(
        on_device, mesh=mesh, in_specs=placed, out_specs=P(("dp", "seq"), None), check_vma=False
    )
```

```python
import functools
import math

import jax
import jax.numpy as jnp
from jax import lax
from jax.experimental import pallas as pl
from jax.experimental.pallas import tpu as pltpu
from jax.sharding import PartitionSpec as P

HEAD = 128
TOK = 256
OWNERS = 64
CELL = 8
SLOTS = OWNERS * CELL
HEADS = 16
CARRIED = 2 * HEADS
CHUNKS = 2
HPC = HEADS // CHUNKS
COMPACT = 96
GROUP = 32
FILLS = 2
EMPTY = 128.0
VMEM = 48 * 1024 * 1024
BF = jnp.bfloat16
F32 = jnp.float32


def dot(a, b, dims):
    return lax.dot_general(a, b, (dims, ((), ())), preferred_element_type=F32)


NN = ((1,), (0,))
NT = ((1,), (1,))


def params(*semantics, vmem=VMEM):
    return pltpu.CompilerParams(vmem_limit_bytes=vmem, dimension_semantics=semantics or None)


def slot_kernel(col_ref, row_ref, out_ref, held_ref, row_of_ref, over_ref):
    earlier = lax.broadcasted_iota(jnp.int32, (TOK, TOK), 0) < lax.broadcasted_iota(
        jnp.int32, (TOK, TOK), 1
    )
    owners = lax.broadcasted_iota(jnp.int32, (OWNERS, TOK), 0)
    lanes = lax.broadcasted_iota(jnp.int32, (HEADS * CELL, TOK), 0)
    held = None
    for h in range(HEADS):
        row = row_ref[h : h + 1, :]
        same = (col_ref[:, h : h + 1] == row) & earlier
        rank = jnp.sum(jnp.where(same, 1, 0), axis=0, keepdims=True)
        owner = (row + 4 * h + row // OWNERS) % OWNERS
        cell = (row // OWNERS) * 2 + rank
        out_ref[h : h + 1, :] = owner * CELL + cell
        to_owner = jnp.where(owners == owner, 1.0, 0.0).astype(BF)
        to_lane = jnp.where(lanes == h * CELL + cell, 1.0, 0.0).astype(BF)
        term = dot(to_owner, to_lane, NT)
        held = term if held is None else held + term
    held_ref[...] = held
    before = lax.broadcasted_iota(jnp.int32, (HEADS * CELL, HEADS * CELL), 0) < (
        lax.broadcasted_iota(jnp.int32, (HEADS * CELL, HEADS * CELL), 1)
    )
    rank = dot(held.astype(BF), jnp.where(before, 1.0, 0.0).astype(BF), NN)
    row_of = jnp.where(held > 0.5, rank + 1.0, -1.0)
    row_of_ref[...] = row_of
    most = jnp.max(jnp.max(row_of, axis=0, keepdims=True), axis=1, keepdims=True)
    over_ref[...] = jnp.broadcast_to(jnp.where(most >= COMPACT, 1.0, 0.0), over_ref.shape)


def slots_of(assign):
    per_owner = jax.ShapeDtypeStruct((OWNERS, HEADS * CELL), F32)
    return pl.pallas_call(
        slot_kernel,
        out_shape=(
            jax.ShapeDtypeStruct((HEADS, TOK), jnp.int32),
            per_owner,
            per_owner,
            jax.ShapeDtypeStruct((8, HEAD), F32),
        ),
        compiler_params=params(),
        name="slots",
    )(assign, assign.T)


def compact_kernel(slot_ref, row_of_ref, held_ref, flag_ref, one_ref, two_ref, out_ref, buf_ref):
    p = pl.program_id(0)

    @pl.when(p < FILLS)
    def _():
        place = lax.broadcasted_iota(jnp.int32, (SLOTS, TOK), 0)
        for e in range(0, HEADS // FILLS, 2):
            parts = []
            for h in (e, e + 1):
                hot = jnp.where(place == slot_ref[0, h : h + 1, :], 1.0, 0.0).astype(BF)
                here = slice(h * HEAD, (h + 1) * HEAD)
                both = jnp.concatenate([one_ref[:, here], two_ref[:, here]], axis=1)
                parts.append(dot(hot, both, NN).reshape(OWNERS, CELL, 2 * HEAD))
            first = p * (HEADS // FILLS) * CELL + e * CELL
            at = pl.ds(pl.multiple_of(first, 2 * CELL), 2 * CELL)
            buf_ref[:, at, :] = jnp.concatenate(parts, axis=1).astype(BF)

    @pl.when(p >= FILLS)
    def _():
        first = pl.multiple_of((p - FILLS) * GROUP, GROUP)
        row_of = row_of_ref[pl.ds(first, GROUP), :]
        row_of = jnp.where(row_of < COMPACT, row_of, -2.0 * COMPACT).astype(jnp.int32)
        held = held_ref[pl.ds(first, GROUP), :]
        notes = jnp.concatenate([held, jnp.broadcast_to(flag_ref[0:1, :], held.shape)], axis=1)
        place = lax.broadcasted_iota(jnp.int32, (2 * COMPACT, 2 * HEAD), 0)
        line = lax.broadcasted_iota(jnp.int32, (2 * CELL, 2 * HEAD), 0)
        for d in range(0, GROUP, 2):
            target = jnp.concatenate([row_of[d : d + 1], row_of[d + 1 : d + 2] + COMPACT], axis=1)
            hot = jnp.where(place == target, 1.0, 0.0).astype(BF)
            rows = buf_ref[pl.ds(first + d, 2)].reshape(2 * HEADS * CELL, 2 * HEAD)
            block = dot(hot, rows, NN)
            for e in range(2):
                mine = block[e * COMPACT : (e + 1) * COMPACT]
                top = jnp.where(line == 0, notes[d + e : d + e + 1], mine[: 2 * CELL])
                out_ref[d + e] = jnp.concatenate([top, mine[2 * CELL :]], axis=0).astype(BF)


def compact(slots, row_of, held, flag, one, two):
    groups = OWNERS // GROUP
    share = HEADS // FILLS
    whole = pl.BlockSpec((OWNERS, HEADS * CELL), lambda p: (0, 0))
    source = pl.BlockSpec((TOK, share * HEAD), lambda p: (0, jnp.minimum(p, FILLS - 1)))
    return pl.pallas_call(
        compact_kernel,
        grid=(FILLS + groups,),
        in_specs=[
            pl.BlockSpec((1, share, TOK), lambda p: (jnp.minimum(p, FILLS - 1), 0, 0)),
            whole,
            whole,
            pl.BlockSpec((8, HEAD), lambda p: (0, 0)),
            source,
            source,
        ],
        out_specs=pl.BlockSpec(
            (GROUP, COMPACT, 2 * HEAD), lambda p: (jnp.maximum(p - FILLS, 0), 0, 0)
        ),
        out_shape=jax.ShapeDtypeStruct((OWNERS, COMPACT, 2 * HEAD), BF),
        scratch_shapes=[pltpu.VMEM((OWNERS, HEADS * CELL, 2 * HEAD), BF)],
        compiler_params=params("arbitrary", vmem=60 * 1024 * 1024),
        cost_estimate=pl.CostEstimate(
            flops=4 * 2**30, bytes_accessed=8 * 2**20, transcendentals=0
        ),
        name="compact",
    )(slots.reshape(FILLS, share, TOK), row_of, held, flag, one, two)


def spread_kernel(mark, got_ref, note_ref, out_ref, flag_ref):
    notes = got_ref[:, : 2 * CELL, HEAD:].astype(F32)[:, 0, :]
    flag = jnp.broadcast_to(jnp.max(notes, axis=0, keepdims=True), flag_ref.shape)

    @pl.when(pl.program_id(0) == 0)
    def _():
        flag_ref[...] = flag

    @pl.when(pl.program_id(0) > 0)
    def _():
        flag_ref[...] = jnp.maximum(flag_ref[...], flag)

    slots = HEADS * CELL
    row = lax.broadcasted_iota(jnp.int32, (slots, slots), 0)
    col = lax.broadcasted_iota(jnp.int32, (slots, slots), 1)
    held = note_ref[...].astype(F32)[:, 0, :HEAD].astype(BF)
    rank = dot(jnp.where(col < row, 1.0, 0.0).astype(BF), held, NT)
    is_held = dot(jnp.where(col == row, 1.0, 0.0).astype(BF), held, NT) > 0.5
    target = jnp.where(is_held, rank + 1.0, -2.0 * COMPACT).astype(jnp.int32)
    place = lax.broadcasted_iota(jnp.int32, (2 * slots, 2 * COMPACT), 1)
    for s in range(0, GROUP, 2):
        goal = jnp.concatenate([target[:, s : s + 1], target[:, s + 1 : s + 2] + COMPACT], axis=0)
        hot = jnp.where(place == goal, 1.0, 0.0).astype(BF)
        rows = dot(hot, got_ref[s : s + 2].reshape(2 * COMPACT, 2 * HEAD), NN)
        if mark:
            rows = jnp.concatenate(
                [jnp.where(goal > 0, rows[:, :HEAD], EMPTY), rows[:, HEAD:]], axis=1
            )
        out_ref[s : s + 2] = rows.reshape(2, slots, 2 * HEAD).astype(BF)


def spread(got, notes, mark):
    return pl.pallas_call(
        functools.partial(spread_kernel, mark),
        grid=(OWNERS // GROUP,),
        in_specs=[
            pl.BlockSpec((GROUP, COMPACT, 2 * HEAD), lambda p: (p, 0, 0)),
            pl.BlockSpec((GROUP, 2 * CELL, 2 * HEAD), lambda p: (p, 0, 0)),
        ],
        out_specs=(
            pl.BlockSpec((GROUP, HEADS * CELL, 2 * HEAD), lambda p: (p, 0, 0)),
            pl.BlockSpec((8, HEAD), lambda p: (0, 0)),
        ),
        out_shape=(
            jax.ShapeDtypeStruct((OWNERS, HEADS * CELL, 2 * HEAD), BF),
            jax.ShapeDtypeStruct((8, HEAD), F32),
        ),
        compiler_params=params("arbitrary"),
        cost_estimate=pl.CostEstimate(
            flops=2 * 2**30, bytes_accessed=8 * 2**20, transcendentals=0
        ),
        name="spread",
    )(got, notes)


def pack_kernel(mark, slot_ref, *refs):
    sources, out_ref = refs[:-1], refs[-1]
    place = lax.broadcasted_iota(jnp.int32, (SLOTS, TOK), 0)
    for n, source in enumerate(sources):
        parts = []
        for e in range(2):
            hot = jnp.where(place == slot_ref[0, e : e + 1, :], 1.0, 0.0)
            hot_low = hot.astype(BF)
            rows = dot(hot_low, source[:, e * HEAD : (e + 1) * HEAD], NN)
            if mark and n == 0:
                filled = dot(hot_low, jnp.ones((TOK, HEAD), BF), NN)
                rows = jnp.where(filled > 0.5, rows, EMPTY)
            parts.append(rows.reshape(OWNERS, CELL, HEAD))
        out_ref[:, :, n * HEAD : (n + 1) * HEAD] = jnp.concatenate(parts, axis=1).astype(BF)


def pack(slots, chunk, mark, *sources):
    pairs = HPC // 2
    width = HEAD * len(sources)
    return pl.pallas_call(
        functools.partial(pack_kernel, mark),
        grid=(pairs,),
        in_specs=[pl.BlockSpec((1, 2, TOK), lambda p: (chunk * pairs + p, 0, 0))]
        + [pl.BlockSpec((TOK, 2 * HEAD), lambda p: (0, chunk * pairs + p)) for _ in sources],
        out_specs=pl.BlockSpec((OWNERS, 2 * CELL, width), lambda p: (0, p, 0)),
        out_shape=jax.ShapeDtypeStruct((OWNERS, HPC * CELL, width), BF),
        compiler_params=params("arbitrary"),
        cost_estimate=pl.CostEstimate(
            flops=2 * HPC * SLOTS * TOK * width * 4, bytes_accessed=6 * 2**20, transcendentals=0
        ),
        name="pack",
    )(slots.reshape(HEADS // 2, 2, TOK), *sources)


def attention_kernel(kv_ref, gq_ref, out_ref, bias_ref):
    scale = 1.0 / math.sqrt(HEAD)
    to_exp2 = scale * math.log2(math.e)

    @pl.when(pl.program_id(0) == 0)
    def _():
        row = lax.broadcasted_iota(jnp.int32, (SLOTS, SLOTS), 0)
        col = lax.broadcasted_iota(jnp.int32, (SLOTS, SLOTS), 1)
        keep = (col <= row) & ((row % CELL) // 2 == (col % CELL) // 2)
        bias_ref[...] = jnp.where(keep, 0.0, -1e30)

    first = jnp.where(lax.broadcasted_iota(jnp.int32, (8, HEAD), 1) == 0, 1.0, 0.0).astype(BF)
    def halves(ref):
        pair = ref[...].astype(F32)
        heads = [pair[:, e * CELL : (e + 1) * CELL, :].reshape(SLOTS, 2 * HEAD) for e in range(2)]
        return [x[:, n * HEAD : (n + 1) * HEAD].astype(BF) for n in range(2) for x in heads]

    both = range(2)
    k, v = (lambda x: (x[:2], x[2:]))(halves(kv_ref))
    g, q = (lambda x: (x[:2], x[2:]))(halves(gq_ref))
    key_bias = [
        jnp.where(dot(first, k[e], NT)[0:1, :] > 0.5 * EMPTY, -1e30, 0.0) for e in both
    ]
    scores = [dot(q[e], k[e], NT) for e in both]
    dweights = [dot(g[e], v[e], NT) for e in both]
    raised = [jnp.exp2(scores[e] * to_exp2 + bias_ref[...] + key_bias[e]) for e in both]
    totals = [jnp.sum(raised[e], axis=1, keepdims=True) for e in both]
    weights = [raised[e] * (1.0 / jnp.where(totals[e] == 0.0, 1.0, totals[e])) for e in both]
    attended = [dot(weights[e].astype(BF), v[e], NN) for e in both]
    delta = [jnp.sum(g[e].astype(F32) * attended[e], axis=1, keepdims=True) for e in both]
    dscores = [(weights[e] * (dweights[e] - delta[e])).astype(BF) for e in both]
    for e in both:
        dquery = (dot(dscores[e], k[e], NN) * scale).astype(BF)
        at = slice(e * 2 * CELL, (e + 1) * 2 * CELL)
        out_ref[0, :, 0, at] = dquery.reshape(OWNERS // 2, 2 * CELL, HEAD)


def attention(kv, gq):
    def pair_spec():
        return pl.BlockSpec((OWNERS, 2 * CELL, 2 * HEAD), lambda p: (0, p, 0))

    groups = HEADS // 2
    return pl.pallas_call(
        attention_kernel,
        grid=(groups,),
        in_specs=[pair_spec(), pair_spec()],
        out_specs=pl.BlockSpec(
            (1, OWNERS // 2, 1, 4 * CELL, HEAD), lambda p: (p // 2, 0, p % 2, 0, 0)
        ),
        out_shape=jax.ShapeDtypeStruct((groups // 2, OWNERS // 2, 2, 4 * CELL, HEAD), BF),
        scratch_shapes=[pltpu.VMEM((SLOTS, SLOTS), F32)],
        compiler_params=params("arbitrary", vmem=63 * 1024 * 1024),
        cost_estimate=pl.CostEstimate(
            flops=HEADS * 8 * SLOTS * SLOTS * HEAD,
            bytes_accessed=10 * 2**20,
            transcendentals=HEADS * SLOTS * SLOTS,
        ),
        name="attention",
    )(kv, gq)


def grad_kernel(where_ref, rows_ref, act_a, act_b, out_ref, acc_ref):
    b = pl.program_id(0)
    group, core = where_ref[0], where_ref[1]
    features = acc_ref.shape[0]
    rows = rows_ref[...].astype(F32)
    parts = [rows[:, n * CELL : (n + 1) * CELL].reshape(SLOTS, HEAD) for n in range(4)]
    line = lax.broadcasted_iota(jnp.int32, (2 * HEADS, TOK), 0)
    place = lax.broadcasted_iota(jnp.int32, (SLOTS, TOK), 0)
    total = None
    for act_ref, side in ((act_a, core), (act_b, 1 - core)):
        slot = act_ref[0, features:, :].astype(F32)
        dquery = []
        for e in range(2):
            head = 2 * group + e
            mine = jnp.where(side == 0, parts[2 * e], parts[2 * e + 1]).astype(BF)
            weight = jnp.where(line == head, 1.0 * CELL, jnp.where(line == HEADS + head, 1.0, 0.0))
            index = jnp.sum(slot * weight, axis=0, keepdims=True).astype(jnp.int32)
            hot = jnp.where(place == index, 1.0, 0.0).astype(BF)
            dquery.append(dot(mine, hot, ((0,), (0,))))
        dquery = jnp.concatenate(dquery, axis=0).astype(BF)
        term = dot(act_ref[0, :features, :], dquery, NT)
        total = term if total is None else total + term

    @pl.when(b == 0)
    def _():
        acc_ref[...] = total

    @pl.when(b > 0)
    def _():
        acc_ref[...] += total

    @pl.when(b == pl.num_programs(0) - 1)
    def _():
        both = [acc_ref[:, e * HEAD : (e + 1) * HEAD].reshape(-1, CELL, HEAD) for e in range(2)]
        out_ref[...] = jnp.concatenate(both, axis=1).astype(BF)


def weight_grad(where, rows, acts, features, seqs):
    def act_spec():
        return pl.BlockSpec((1, features + CARRIED, TOK), lambda b, w: (b, 0, 0))

    out = (features // CELL, 2 * CELL, HEAD)
    return pl.pallas_call(
        grad_kernel,
        grid_spec=pltpu.PrefetchScalarGridSpec(
            num_scalar_prefetch=1,
            grid=(seqs,),
            in_specs=[
                pl.BlockSpec((OWNERS, 4 * CELL, HEAD), lambda b, w: (b, 0, 0)),
                act_spec(),
                act_spec(),
            ],
            out_specs=pl.BlockSpec(out, lambda b, w: (0, 0, 0)),
            scratch_shapes=[pltpu.VMEM((features, 2 * HEAD), F32)],
        ),
        out_shape=jax.ShapeDtypeStruct(out, BF),
        compiler_params=params("arbitrary"),
        cost_estimate=pl.CostEstimate(
            flops=8 * seqs * TOK * features * HEAD * 2,
            bytes_accessed=12 * 2**20,
            transcendentals=0,
        ),
        name="weight_grad",
    )(where, rows, *acts)


def on_device(activations, w_query, all_keys, values, grad_out, cluster):
    tokens_here = activations[0]
    features = tokens_here.shape[1]
    seqs = lax.axis_size("dp")
    devices = seqs * OWNERS
    slots, held, row_of, over = slots_of(cluster[0])
    seq_send = functools.partial(
        lax.all_to_all, axis_name="seq", split_axis=0, concat_axis=0, tiled=True
    )
    all_send = functools.partial(
        lax.all_to_all, axis_name=("dp", "seq"), split_axis=0, concat_axis=0, tiled=True
    )
    keys, vals, grads = all_keys[0], values[0], grad_out[0]

    core = lax.axis_index("seq") % 2
    group = lax.axis_index("dp") * 2 + core
    flag = over
    for shift in range(1, seqs):
        ring = [(i, (i + shift) % seqs) for i in range(seqs)]
        flag = jnp.maximum(flag, lax.ppermute(over, "dp", ring))

    got_kv = seq_send(compact(slots, row_of, held, jnp.zeros((8, HEAD), F32), keys, vals))
    queries = jnp.dot(tokens_here, w_query, preferred_element_type=F32).astype(BF)
    send_gq = compact(slots, row_of, held, flag, grads, queries)
    carried = jnp.concatenate(
        [tokens_here.T, (slots // CELL).astype(BF), (slots % CELL).astype(BF)], axis=0
    )
    send_gq, got_kv, carried = lax.optimization_barrier((send_gq, got_kv, carried))
    got_gq = seq_send(send_gq)

    acts_mine = lax.all_gather(carried, "dp")
    acts = (acts_mine, lax.ppermute(acts_mine, "seq", [(i, i ^ 1) for i in range(OWNERS)]))

    def send_all_slots(state):
        def whole(mark, *sources):
            parts = [pack(slots, c, mark, *sources) for c in range(CHUNKS)]
            return seq_send(jnp.concatenate(parts, axis=1))

        return jnp.zeros_like(state[0]), whole(True, keys, vals), whole(False, grads, queries)

    kv, _ = spread(got_kv, got_kv, True)
    gq, flags = spread(got_gq, got_kv, False)
    _, kv, gq = lax.while_loop(
        lambda state: state[0] > 0.5, send_all_slots, (flags[0, 0], kv, gq)
    )
    back = all_send(attention(kv, gq).reshape(devices, 4 * CELL, HEAD))
    where = jnp.stack([group, core]).astype(jnp.int32)
    terms = all_send(weight_grad(where, back, acts, features, seqs))
    terms = terms.reshape(seqs, OWNERS // 2, 2, 2, features // devices, HEAD)
    out = jnp.sum(terms.astype(F32), axis=1)
    out = out.transpose(3, 0, 1, 2, 4)
    return out.reshape(features // devices, HEADS * HEAD)


def solution(mesh):
    placed = (
        P("dp", "seq", None),
        P(),
        P("dp", "seq", None),
        P("dp", "seq", None),
        P("dp", "seq", None),
        P("dp", "seq", None),
    )
    return jax.shard_map(
        on_device, mesh=mesh, in_specs=placed, out_specs=P(("dp", "seq"), None), check_vma=False
    )
```

```python
import functools
import math

import jax
import jax.numpy as jnp
from jax import lax
from jax.experimental import pallas as pl
from jax.experimental.pallas import tpu as pltpu
from jax.sharding import PartitionSpec as P

HEAD = 128
TOK = 256
OWNERS = 64
CELL = 8
SLOTS = OWNERS * CELL
HEADS = 16
CARRIED = 2 * HEADS
CHUNKS = 2
HPC = HEADS // CHUNKS
COMPACT = 96
GROUP = 32
FILLS = 2
EMPTY = 128.0
VMEM = 48 * 1024 * 1024
BF = jnp.bfloat16
F32 = jnp.float32


def dot(a, b, dims):
    return lax.dot_general(a, b, (dims, ((), ())), preferred_element_type=F32)


NN = ((1,), (0,))
NT = ((1,), (1,))


def params(*semantics, vmem=VMEM):
    return pltpu.CompilerParams(vmem_limit_bytes=vmem, dimension_semantics=semantics or None)


def slot_kernel(col_ref, row_ref, out_ref, row_of_ref, over_ref):
    earlier = lax.broadcasted_iota(jnp.int32, (TOK, TOK), 0) < lax.broadcasted_iota(
        jnp.int32, (TOK, TOK), 1
    )
    owners = lax.broadcasted_iota(jnp.int32, (OWNERS, TOK), 0)
    lanes = lax.broadcasted_iota(jnp.int32, (HEADS * CELL, TOK), 0)
    held = None
    for h in range(HEADS):
        row = row_ref[h : h + 1, :]
        same = (col_ref[:, h : h + 1] == row) & earlier
        rank = jnp.sum(jnp.where(same, 1, 0), axis=0, keepdims=True)
        owner = (row + 4 * h + row // OWNERS) % OWNERS
        cell = (row // OWNERS) * 2 + rank
        out_ref[h : h + 1, :] = owner * CELL + cell
        to_owner = jnp.where(owners == owner, 1.0, 0.0).astype(BF)
        to_lane = jnp.where(lanes == h * CELL + cell, 1.0, 0.0).astype(BF)
        term = dot(to_owner, to_lane, NT)
        held = term if held is None else held + term
    before = lax.broadcasted_iota(jnp.int32, (HEADS * CELL, HEADS * CELL), 0) < (
        lax.broadcasted_iota(jnp.int32, (HEADS * CELL, HEADS * CELL), 1)
    )
    rank = dot(held.astype(BF), jnp.where(before, 1.0, 0.0).astype(BF), NN)
    row_of = jnp.where(held > 0.5, rank + 1.0, -1.0)
    row_of_ref[...] = row_of
    most = jnp.max(jnp.max(row_of, axis=0, keepdims=True), axis=1, keepdims=True)
    over_ref[...] = jnp.broadcast_to(jnp.where(most >= COMPACT, 1.0, 0.0), over_ref.shape)


def slots_of(assign):
    per_owner = jax.ShapeDtypeStruct((OWNERS, HEADS * CELL), F32)
    return pl.pallas_call(
        slot_kernel,
        out_shape=(
            jax.ShapeDtypeStruct((HEADS, TOK), jnp.int32),
            per_owner,
            jax.ShapeDtypeStruct((8, HEAD), F32),
        ),
        compiler_params=params(),
        name="slots",
    )(assign, assign.T)


def compact_kernel(slot_ref, row_of_ref, flag_ref, one_ref, two_ref, out_ref, buf_ref):
    p = pl.program_id(0)

    @pl.when(p < FILLS)
    def _():
        place = lax.broadcasted_iota(jnp.int32, (SLOTS, TOK), 0)
        for e in range(0, HEADS // FILLS, 2):
            parts = []
            for h in (e, e + 1):
                hot = jnp.where(place == slot_ref[0, h : h + 1, :], 1.0, 0.0).astype(BF)
                here = slice(h * HEAD, (h + 1) * HEAD)
                both = jnp.concatenate([one_ref[:, here], two_ref[:, here]], axis=1)
                parts.append(dot(hot, both, NN).reshape(OWNERS, CELL, 2 * HEAD))
            first = p * (HEADS // FILLS) * CELL + e * CELL
            at = pl.ds(pl.multiple_of(first, 2 * CELL), 2 * CELL)
            buf_ref[:, at, :] = jnp.concatenate(parts, axis=1).astype(BF)

    @pl.when(p >= FILLS)
    def _():
        first = pl.multiple_of((p - FILLS) * GROUP, GROUP)
        row_of = row_of_ref[pl.ds(first, GROUP), :]
        held = jnp.where(row_of > 0.5, 1.0, 0.0)
        row_of = jnp.where(row_of < COMPACT, row_of, -2.0 * COMPACT).astype(jnp.int32)
        notes = jnp.concatenate([held, jnp.broadcast_to(flag_ref[0:1, :], held.shape)], axis=1)
        place = lax.broadcasted_iota(jnp.int32, (2 * COMPACT, 2 * HEAD), 0)
        line = lax.broadcasted_iota(jnp.int32, (2 * CELL, 2 * HEAD), 0)
        for d in range(0, GROUP, 2):
            target = jnp.concatenate([row_of[d : d + 1], row_of[d + 1 : d + 2] + COMPACT], axis=1)
            hot = jnp.where(place == target, 1.0, 0.0).astype(BF)
            rows = buf_ref[pl.ds(first + d, 2)].reshape(2 * HEADS * CELL, 2 * HEAD)
            block = dot(hot, rows, NN)
            for e in range(2):
                mine = block[e * COMPACT : (e + 1) * COMPACT]
                top = jnp.where(line == 0, notes[d + e : d + e + 1], mine[: 2 * CELL])
                out_ref[d + e] = jnp.concatenate([top, mine[2 * CELL :]], axis=0).astype(BF)


def compact(slots, row_of, flag, one, two):
    groups = OWNERS // GROUP
    share = HEADS // FILLS
    whole = pl.BlockSpec((OWNERS, HEADS * CELL), lambda p: (0, 0))
    source = pl.BlockSpec((TOK, share * HEAD), lambda p: (0, jnp.minimum(p, FILLS - 1)))
    return pl.pallas_call(
        compact_kernel,
        grid=(FILLS + groups,),
        in_specs=[
            pl.BlockSpec((1, share, TOK), lambda p: (jnp.minimum(p, FILLS - 1), 0, 0)),
            whole,
            pl.BlockSpec((8, HEAD), lambda p: (0, 0)),
            source,
            source,
        ],
        out_specs=pl.BlockSpec(
            (GROUP, COMPACT, 2 * HEAD), lambda p: (jnp.maximum(p - FILLS, 0), 0, 0)
        ),
        out_shape=jax.ShapeDtypeStruct((OWNERS, COMPACT, 2 * HEAD), BF),
        scratch_shapes=[pltpu.VMEM((OWNERS, HEADS * CELL, 2 * HEAD), BF)],
        compiler_params=params("arbitrary", vmem=60 * 1024 * 1024),
        cost_estimate=pl.CostEstimate(
            flops=4 * 2**30, bytes_accessed=8 * 2**20, transcendentals=0
        ),
        name="compact",
    )(slots.reshape(FILLS, share, TOK), row_of, flag, one, two)


def spread_kernel(mark, got_ref, note_ref, out_ref, flag_ref):
    notes = got_ref[:, : 2 * CELL, HEAD:].astype(F32)[:, 0, :]
    flag = jnp.broadcast_to(jnp.max(notes, axis=0, keepdims=True), flag_ref.shape)

    @pl.when(pl.program_id(0) == 0)
    def _():
        flag_ref[...] = flag

    @pl.when(pl.program_id(0) > 0)
    def _():
        flag_ref[...] = jnp.maximum(flag_ref[...], flag)

    slots = HEADS * CELL
    row = lax.broadcasted_iota(jnp.int32, (slots, slots), 0)
    col = lax.broadcasted_iota(jnp.int32, (slots, slots), 1)
    held = note_ref[...].astype(F32)[:, 0, :HEAD].astype(BF)
    rank = dot(jnp.where(col < row, 1.0, 0.0).astype(BF), held, NT)
    is_held = dot(jnp.where(col == row, 1.0, 0.0).astype(BF), held, NT) > 0.5
    target = jnp.where(is_held, rank + 1.0, -2.0 * COMPACT).astype(jnp.int32)
    place = lax.broadcasted_iota(jnp.int32, (2 * slots, 2 * COMPACT), 1)
    for s in range(0, GROUP, 2):
        goal = jnp.concatenate([target[:, s : s + 1], target[:, s + 1 : s + 2] + COMPACT], axis=0)
        hot = jnp.where(place == goal, 1.0, 0.0).astype(BF)
        rows = dot(hot, got_ref[s : s + 2].reshape(2 * COMPACT, 2 * HEAD), NN)
        if mark:
            rows = jnp.concatenate(
                [jnp.where(goal > 0, rows[:, :HEAD], EMPTY), rows[:, HEAD:]], axis=1
            )
        out_ref[s : s + 2] = rows.reshape(2, slots, 2 * HEAD).astype(BF)


def spread(got, notes, mark):
    return pl.pallas_call(
        functools.partial(spread_kernel, mark),
        grid=(OWNERS // GROUP,),
        in_specs=[
            pl.BlockSpec((GROUP, COMPACT, 2 * HEAD), lambda p: (p, 0, 0)),
            pl.BlockSpec((GROUP, 2 * CELL, 2 * HEAD), lambda p: (p, 0, 0)),
        ],
        out_specs=(
            pl.BlockSpec((GROUP, HEADS * CELL, 2 * HEAD), lambda p: (p, 0, 0)),
            pl.BlockSpec((8, HEAD), lambda p: (0, 0)),
        ),
        out_shape=(
            jax.ShapeDtypeStruct((OWNERS, HEADS * CELL, 2 * HEAD), BF),
            jax.ShapeDtypeStruct((8, HEAD), F32),
        ),
        compiler_params=params("arbitrary"),
        cost_estimate=pl.CostEstimate(
            flops=2 * 2**30, bytes_accessed=8 * 2**20, transcendentals=0
        ),
        name="spread",
    )(got, notes)


def pack_kernel(mark, slot_ref, *refs):
    sources, out_ref = refs[:-1], refs[-1]
    place = lax.broadcasted_iota(jnp.int32, (SLOTS, TOK), 0)
    for n, source in enumerate(sources):
        parts = []
        for e in range(2):
            hot = jnp.where(place == slot_ref[0, e : e + 1, :], 1.0, 0.0)
            hot_low = hot.astype(BF)
            rows = dot(hot_low, source[:, e * HEAD : (e + 1) * HEAD], NN)
            if mark and n == 0:
                filled = dot(hot_low, jnp.ones((TOK, HEAD), BF), NN)
                rows = jnp.where(filled > 0.5, rows, EMPTY)
            parts.append(rows.reshape(OWNERS, CELL, HEAD))
        out_ref[:, :, n * HEAD : (n + 1) * HEAD] = jnp.concatenate(parts, axis=1).astype(BF)


def pack(slots, chunk, mark, *sources):
    pairs = HPC // 2
    width = HEAD * len(sources)
    return pl.pallas_call(
        functools.partial(pack_kernel, mark),
        grid=(pairs,),
        in_specs=[pl.BlockSpec((1, 2, TOK), lambda p: (chunk * pairs + p, 0, 0))]
        + [pl.BlockSpec((TOK, 2 * HEAD), lambda p: (0, chunk * pairs + p)) for _ in sources],
        out_specs=pl.BlockSpec((OWNERS, 2 * CELL, width), lambda p: (0, p, 0)),
        out_shape=jax.ShapeDtypeStruct((OWNERS, HPC * CELL, width), BF),
        compiler_params=params("arbitrary"),
        cost_estimate=pl.CostEstimate(
            flops=2 * HPC * SLOTS * TOK * width * 4, bytes_accessed=6 * 2**20, transcendentals=0
        ),
        name="pack",
    )(slots.reshape(HEADS // 2, 2, TOK), *sources)


def attention_kernel(kv_ref, gq_ref, out_ref, bias_ref):
    scale = 1.0 / math.sqrt(HEAD)
    to_exp2 = scale * math.log2(math.e)

    @pl.when(pl.program_id(0) == 0)
    def _():
        row = lax.broadcasted_iota(jnp.int32, (SLOTS, SLOTS), 0)
        col = lax.broadcasted_iota(jnp.int32, (SLOTS, SLOTS), 1)
        keep = (col <= row) & ((row % CELL) // 2 == (col % CELL) // 2)
        bias_ref[...] = jnp.where(keep, 0.0, -1e30)

    first = jnp.where(lax.broadcasted_iota(jnp.int32, (8, HEAD), 1) == 0, 1.0, 0.0).astype(BF)
    def halves(ref):
        pair = ref[...].astype(F32)
        heads = [pair[:, e * CELL : (e + 1) * CELL, :].reshape(SLOTS, 2 * HEAD) for e in range(2)]
        return [x[:, n * HEAD : (n + 1) * HEAD].astype(BF) for n in range(2) for x in heads]

    both = range(2)
    k, v = (lambda x: (x[:2], x[2:]))(halves(kv_ref))
    g, q = (lambda x: (x[:2], x[2:]))(halves(gq_ref))
    key_bias = [
        jnp.where(dot(first, k[e], NT)[0:1, :] > 0.5 * EMPTY, -1e30, 0.0) for e in both
    ]
    scores = [dot(q[e], k[e], NT) for e in both]
    dweights = [dot(g[e], v[e], NT) for e in both]
    raised = [jnp.exp2(scores[e] * to_exp2 + bias_ref[...] + key_bias[e]) for e in both]
    totals = [jnp.sum(raised[e], axis=1, keepdims=True) for e in both]
    weights = [raised[e] * (1.0 / jnp.where(totals[e] == 0.0, 1.0, totals[e])) for e in both]
    attended = [dot(weights[e].astype(BF), v[e], NN) for e in both]
    delta = [jnp.sum(g[e].astype(F32) * attended[e], axis=1, keepdims=True) for e in both]
    dscores = [(weights[e] * (dweights[e] - delta[e])).astype(BF) for e in both]
    for e in both:
        dquery = (dot(dscores[e], k[e], NN) * scale).astype(BF)
        at = slice(e * 2 * CELL, (e + 1) * 2 * CELL)
        out_ref[0, :, 0, at] = dquery.reshape(OWNERS // 2, 2 * CELL, HEAD)


def attention(kv, gq):
    def pair_spec():
        return pl.BlockSpec((OWNERS, 2 * CELL, 2 * HEAD), lambda p: (0, p, 0))

    groups = HEADS // 2
    return pl.pallas_call(
        attention_kernel,
        grid=(groups,),
        in_specs=[pair_spec(), pair_spec()],
        out_specs=pl.BlockSpec(
            (1, OWNERS // 2, 1, 4 * CELL, HEAD), lambda p: (p // 2, 0, p % 2, 0, 0)
        ),
        out_shape=jax.ShapeDtypeStruct((groups // 2, OWNERS // 2, 2, 4 * CELL, HEAD), BF),
        scratch_shapes=[pltpu.VMEM((SLOTS, SLOTS), F32)],
        compiler_params=params("arbitrary", vmem=63 * 1024 * 1024),
        cost_estimate=pl.CostEstimate(
            flops=HEADS * 8 * SLOTS * SLOTS * HEAD,
            bytes_accessed=10 * 2**20,
            transcendentals=HEADS * SLOTS * SLOTS,
        ),
        name="attention",
    )(kv, gq)


def grad_kernel(where_ref, rows_ref, act_a, act_b, out_ref, acc_ref):
    b = pl.program_id(0)
    group, core = where_ref[0], where_ref[1]
    features = acc_ref.shape[0]
    rows = rows_ref[...].astype(F32)
    parts = [rows[:, n * CELL : (n + 1) * CELL].reshape(SLOTS, HEAD) for n in range(4)]
    line = lax.broadcasted_iota(jnp.int32, (2 * HEADS, TOK), 0)
    place = lax.broadcasted_iota(jnp.int32, (SLOTS, TOK), 0)
    total = None
    for act_ref, side in ((act_a, core), (act_b, 1 - core)):
        slot = act_ref[0, features:, :].astype(F32)
        dquery = []
        for e in range(2):
            head = 2 * group + e
            mine = jnp.where(side == 0, parts[2 * e], parts[2 * e + 1]).astype(BF)
            weight = jnp.where(line == head, 1.0 * CELL, jnp.where(line == HEADS + head, 1.0, 0.0))
            index = jnp.sum(slot * weight, axis=0, keepdims=True).astype(jnp.int32)
            hot = jnp.where(place == index, 1.0, 0.0).astype(BF)
            dquery.append(dot(mine, hot, ((0,), (0,))))
        dquery = jnp.concatenate(dquery, axis=0).astype(BF)
        term = dot(act_ref[0, :features, :], dquery, NT)
        total = term if total is None else total + term

    @pl.when(b == 0)
    def _():
        acc_ref[...] = total

    @pl.when(b > 0)
    def _():
        acc_ref[...] += total

    @pl.when(b == pl.num_programs(0) - 1)
    def _():
        both = [acc_ref[:, e * HEAD : (e + 1) * HEAD].reshape(-1, CELL, HEAD) for e in range(2)]
        out_ref[...] = jnp.concatenate(both, axis=1).astype(BF)


def weight_grad(where, rows, acts, features, seqs):
    def act_spec():
        return pl.BlockSpec((1, features + CARRIED, TOK), lambda b, w: (b, 0, 0))

    out = (features // CELL, 2 * CELL, HEAD)
    return pl.pallas_call(
        grad_kernel,
        grid_spec=pltpu.PrefetchScalarGridSpec(
            num_scalar_prefetch=1,
            grid=(seqs,),
            in_specs=[
                pl.BlockSpec((OWNERS, 4 * CELL, HEAD), lambda b, w: (b, 0, 0)),
                act_spec(),
                act_spec(),
            ],
            out_specs=pl.BlockSpec(out, lambda b, w: (0, 0, 0)),
            scratch_shapes=[pltpu.VMEM((features, 2 * HEAD), F32)],
        ),
        out_shape=jax.ShapeDtypeStruct(out, BF),
        compiler_params=params("arbitrary"),
        cost_estimate=pl.CostEstimate(
            flops=8 * seqs * TOK * features * HEAD * 2,
            bytes_accessed=12 * 2**20,
            transcendentals=0,
        ),
        name="weight_grad",
    )(where, rows, *acts)


def on_device(activations, w_query, all_keys, values, grad_out, cluster):
    tokens_here = activations[0]
    features = tokens_here.shape[1]
    seqs = lax.axis_size("dp")
    devices = seqs * OWNERS
    slots, row_of, over = slots_of(cluster[0])
    seq_send = functools.partial(
        lax.all_to_all, axis_name="seq", split_axis=0, concat_axis=0, tiled=True
    )
    all_send = functools.partial(
        lax.all_to_all, axis_name=("dp", "seq"), split_axis=0, concat_axis=0, tiled=True
    )
    keys, vals, grads = all_keys[0], values[0], grad_out[0]

    core = lax.axis_index("seq") % 2
    group = lax.axis_index("dp") * 2 + core
    flag = over
    for shift in range(1, seqs):
        ring = [(i, (i + shift) % seqs) for i in range(seqs)]
        flag = jnp.maximum(flag, lax.ppermute(over, "dp", ring))

    got_kv = seq_send(compact(slots, row_of, over, keys, vals))
    queries = jnp.dot(tokens_here, w_query, preferred_element_type=F32).astype(BF)
    send_gq = compact(slots, row_of, flag, grads, queries)
    carried = jnp.concatenate(
        [tokens_here.T, (slots // CELL).astype(BF), (slots % CELL).astype(BF)], axis=0
    )
    send_gq, got_kv, carried = lax.optimization_barrier((send_gq, got_kv, carried))
    got_gq = seq_send(send_gq)

    acts_mine = lax.all_gather(carried, "dp")
    acts = (acts_mine, lax.ppermute(acts_mine, "seq", [(i, i ^ 1) for i in range(OWNERS)]))

    def send_all_slots(state):
        def whole(mark, *sources):
            parts = [pack(slots, c, mark, *sources) for c in range(CHUNKS)]
            return seq_send(jnp.concatenate(parts, axis=1))

        return jnp.zeros_like(state[0]), whole(True, keys, vals), whole(False, grads, queries)

    kv, _ = spread(got_kv, got_kv, True)
    gq, flags = spread(got_gq, got_kv, False)
    _, kv, gq = lax.while_loop(
        lambda state: state[0] > 0.5, send_all_slots, (flags[0, 0], kv, gq)
    )
    back = all_send(attention(kv, gq).reshape(devices, 4 * CELL, HEAD))
    where = jnp.stack([group, core]).astype(jnp.int32)
    terms = all_send(weight_grad(where, back, acts, features, seqs))
    terms = terms.reshape(seqs, OWNERS // 2, 2, 2, features // devices, HEAD)
    out = jnp.sum(terms.astype(F32), axis=1)
    out = out.transpose(3, 0, 1, 2, 4)
    return out.reshape(features // devices, HEADS * HEAD)


def solution(mesh):
    placed = (
        P("dp", "seq", None),
        P(),
        P("dp", "seq", None),
        P("dp", "seq", None),
        P("dp", "seq", None),
        P("dp", "seq", None),
    )
    return jax.shard_map(
        on_device, mesh=mesh, in_specs=placed, out_specs=P(("dp", "seq"), None), check_vma=False
    )
```
